128 devices in a mesh: pre: 16 (over y, z), head: 8 (over x, core).
Axes of the slice: x: 4, y: 4, z: 4, core: 2. Of those that a mesh axis runs over, the one named last changes fastest.
Arguments:
- query_latent: bfloat16 [640, 128, 576], P('pre', 'head'), may hold values from -12 to 12
- prefix_cache: bfloat16 [80, 512, 576], P('pre'), may hold values from -4 to 4
- block_slot: int32 [10, 8], replicated, may hold values from 0 to 79, as said below
- sample_prompt: int32 [640], replicated, may hold values from 0 to 9, as said below
- suffix_cache: bfloat16 [640, 384, 576], P('pre'), may hold values from -4 to 4
- suffix_length: int32 [640], P('pre'), may hold values from 1 to 384
- value_map: bfloat16 [128, 512, 128], P('head'), may hold values from -3 to 3
- out_weight: bfloat16 [16384, 7168], P('head', 'pre'), may hold values from -0.046875 to 0.046875
Outputs:
- mixed: bfloat16 [640, 7168], P('head', 'pre')
The draws below stay inside these ranges and needn't reach their ends.
Inputs may be any that keep to these rules, and one draw needn't show every extreme that they name: `sample_prompt`: each of the 10 prompts is named by exactly 64 samples. `block_slot`: every slot of prefix_cache is named exactly once.
All inputs are finite; a program needn't handle non-finite values.
Results may differ from the reference program's by a relative error of at most 0.0055.
Values may be sent and summed in bfloat16 or wider, within the bound.
A program may use at most 192 MiB of HBM per device.

```python
import math
import jax
import jax.numpy as jnp
from jax import lax

HEADS = 128
LAT = 512
ROPE = 64
VDIM = 128
D = 7168
GROUP = 64
BLOCK = 512
PBLK = 8
SUF = 384
SAMPLES = 640
PROMPTS = 10
BLOCKS = 80


def layout(key):
    shuffled = jax.random.permutation(jax.random.fold_in(key, 101), SAMPLES)
    sample_prompt = (shuffled // GROUP).astype(jnp.int32)
    block_slot = jax.random.permutation(jax.random.fold_in(key, 102), BLOCKS).astype(jnp.int32).reshape(PROMPTS, PBLK)
    return (sample_prompt, block_slot)


def draw_sample_prompt(key, part):
    shared = layout(key)
    return shared[0]


def draw_block_slot(key, part):
    shared = layout(key)
    return shared[1]


def draw_prefix_cache(key, part):
    key = jax.random.fold_in(key, 3)
    draw_shape = (BLOCKS, BLOCK // 2, 2, LAT + ROPE)
    drawn = jax.random.truncated_normal(key, -4.0, 4.0, draw_shape)
    return drawn.reshape(BLOCKS, BLOCK, LAT + ROPE).astype(jnp.bfloat16)


def draw_query_latent(key, part):
    key = jax.random.fold_in(key, 4)
    drawn = jax.random.truncated_normal(key, -4.0, 4.0, (SAMPLES, HEADS, LAT + ROPE))
    return drawn.astype(jnp.bfloat16)


def draw_suffix_length(key, part):
    key = jax.random.fold_in(key, 10)
    lengths = jax.random.randint(key, (SAMPLES,), 1, SUF + 1)
    lengths = lengths.at[0].set(SUF).at[1].set(1)
    return lengths.astype(jnp.int32)


def shard_levels(rng, shape, shards, smallest, high):
    loudness = 1.0
    for position, shards_of in shards:
        steps = jax.random.uniform(jax.random.fold_in(jax.random.fold_in(rng, 6), position), (shards_of,), jnp.float32, smallest / len(shards), high / len(shards))
        loudness = loudness * jnp.repeat(jnp.exp(steps), shape[position] // shards_of).reshape((-1,) + (1,) * (len(shape) - 1 - position))
    return loudness


def scatter_about(key, extent, width, most, split=(), held_as=jnp.bfloat16):
    values = width * jax.random.normal(key, extent, jnp.float32)
    if split:
        values = values * shard_levels(key, extent, split, -0.22, 0.18)
    return jnp.clip(values, -most, most).astype(held_as)


def setup_inputs(seed: int = 0) -> dict:
    arg_keys = jax.random.split(jax.random.key(seed), 9)
    query_latent = draw_query_latent(jax.random.fold_in(arg_keys[8], 71), 0)
    prefix_cache = draw_prefix_cache(jax.random.fold_in(arg_keys[8], 71), 0)
    block_slot = draw_block_slot(jax.random.fold_in(arg_keys[8], 71), 0)
    sample_prompt = draw_sample_prompt(jax.random.fold_in(arg_keys[8], 71), 0)
    suffix_cache = scatter_about(arg_keys[4], (SAMPLES, SUF, LAT + ROPE), 1.0, 4.0, ((0, 16),))
    suffix_length = draw_suffix_length(jax.random.fold_in(arg_keys[8], 71), 0)
    value_map = scatter_about(arg_keys[6], (HEADS, LAT, VDIM), 0.5, 3.0, ((0, 8),))
    out_weight = scatter_about(arg_keys[7], (HEADS * VDIM, D), (HEADS * VDIM) ** -0.5, 0.046875, ((0, 8), (1, 16)))
    return dict(query_latent=query_latent, prefix_cache=prefix_cache, block_slot=block_slot, sample_prompt=sample_prompt, suffix_cache=suffix_cache, suffix_length=suffix_length, value_map=value_map, out_weight=out_weight)


score_scale = 1.0 / math.sqrt(192.0)
masked_score = -1e+30

def attend(queries, key_rows, live_mask):
    scores = jnp.dot(queries, key_rows.T, preferred_element_type=jnp.float32) * score_scale
    scores = jnp.where(live_mask, scores, masked_score)
    largest = lax.optimization_barrier(jnp.max(scores, axis=1))
    weights = jnp.exp(scores - largest[:, None]).astype(jnp.bfloat16)
    weights = lax.optimization_barrier(weights)
    weight_sum = lax.optimization_barrier(jnp.sum(weights.astype(jnp.float32), axis=1))
    summed = jnp.dot(weights, key_rows[:, :LAT], preferred_element_type=jnp.float32)
    return (summed / weight_sum[:, None], largest + jnp.log(weight_sum))

def merge_pair(first_out, first_lse, second_out, second_lse):
    largest = jnp.maximum(first_lse, second_lse)
    first_weight = jnp.exp(first_lse - largest)
    second_weight = jnp.exp(second_lse - largest)
    weight_sum = first_weight + second_weight
    merged = (first_weight[..., None] * first_out + second_weight[..., None] * second_out) / weight_sum[..., None]
    return (merged, largest + jnp.log(weight_sum))

def reference(query_latent, prefix_cache, block_slot, sample_prompt, suffix_cache, suffix_length, value_map, out_weight):
    members = jnp.argsort(sample_prompt, stable=True).astype(jnp.int32).reshape(PROMPTS, GROUP)
    block_live = jnp.ones((1, BLOCK), bool)

    def one_prompt(prompt):
        member_rows = members[prompt]
        queries = query_latent[member_rows].reshape(GROUP * HEADS, LAT + ROPE)
        merged_out = jnp.zeros((GROUP * HEADS, LAT), jnp.float32)
        merged_lse = jnp.full((GROUP * HEADS,), masked_score, jnp.float32)
        for block_index in range(PBLK):
            block_out, block_lse = attend(queries, prefix_cache[block_slot[prompt, block_index]], block_live)
            merged_out, merged_lse = merge_pair(merged_out, merged_lse, block_out, block_lse)
        return (merged_out.reshape(GROUP, HEADS, LAT), merged_lse.reshape(GROUP, HEADS))
    prompt_out, prompt_lse = lax.map(one_prompt, jnp.arange(PROMPTS, dtype=jnp.int32))
    sample_order = members.reshape(SAMPLES)
    prefix_out = jnp.zeros((SAMPLES, HEADS, LAT), jnp.float32).at[sample_order].set(prompt_out.reshape(SAMPLES, HEADS, LAT))
    prefix_lse = jnp.zeros((SAMPLES, HEADS), jnp.float32).at[sample_order].set(prompt_lse.reshape(SAMPLES, HEADS))
    positions = jnp.arange(SUF, dtype=jnp.int32)

    def one_sample(sample):
        live_mask = (positions < suffix_length[sample])[None, :]
        return attend(query_latent[sample], suffix_cache[sample], live_mask)
    suffix_out, suffix_lse = lax.map(one_sample, jnp.arange(SAMPLES, dtype=jnp.int32))
    latent_out = merge_pair(prefix_out, prefix_lse, suffix_out, suffix_lse)[0]
    heads_out = jnp.einsum('shc,hcv->shv', latent_out, value_map.astype(jnp.float32), precision=lax.Precision.HIGHEST).astype(jnp.bfloat16)
    return jnp.dot(heads_out.reshape(SAMPLES, HEADS * VDIM), out_weight, preferred_element_type=jnp.float32).astype(jnp.bfloat16)
```

```python
import functools
import math

import jax
import jax.numpy as jnp
from jax import lax
from jax.experimental import pallas as pl
from jax.experimental.pallas import tpu as pltpu
from jax.sharding import PartitionSpec as P

GROUP = 64
PRE = 16
HEAD = 8
NS = 40
SP = 48
NH = 16
LAT = 512
VD = 128
SUF = 384
WIN = 80
NSLOT = 5
NPROMPT = 10
NBUF = 4
MASKED = -1e30
SCALE2 = math.log2(math.e) / math.sqrt(192.0)

BF = jnp.bfloat16
F32 = jnp.float32
MESH = pl.DeviceIdType.MESH


def nt(a, b):
    return lax.dot_general(a, b, (((1,), (1,)), ((), ())), preferred_element_type=F32)


def nn(a, b):
    return lax.dot_general(a, b, (((1,), (0,)), ((), ())), preferred_element_type=F32)


def onehot(mask):
    return jnp.where(mask, 1.0, 0.0).astype(BF)


def iota(shape, dim):
    return lax.broadcasted_iota(jnp.int32, shape, dim)


def kernel(
    q_hbm, k_hbm, suf_hbm, vm_hbm, w_hbm, rank_row, rank_col, slots, lens,
    out,
    q_in, k_in, vm, w_in, sufbuf,
    tmat, q_t, qr, sendl, sendr, krl, krr,
    skl, skr, sq, qw, kw, rw,
    lat_s, lt_s, o_s, l_s, osr, lsr, lacc_s,
    ol, op, lps, orr, lr, lacc,
    suf_o, suf_l, hbuf, pb, rs,
    ld_sem, suf_sem, a2a_s, a2a_r, x_s, x_r, c_s, c_r, g1_s, g1_r, g2_s, g2_r, e_s, e_r,
):
    p = lax.axis_index("pre")
    h = lax.axis_index("head")
    x, c = h // 2, lax.rem(h, 2)
    y, z = p // 4, lax.rem(p, 4)
    win, half = p // 2, lax.rem(p, 2)
    wj = lax.rem(win, 4)

    def remote(src, dst, ssem, rsem, pre, head):
        return pltpu.make_async_remote_copy(
            src_ref=src, dst_ref=dst, send_sem=ssem, recv_sem=rsem,
            device_id={"pre": pre, "head": head}, device_id_type=MESH,
        )

    def around(fn):
        def body(d, carry):
            fn(lax.rem(p + d, PRE))
            return carry
        lax.fori_loop(1, PRE, body, 0)

    def lane(i):
        return pl.ds(pl.multiple_of(i * 128, 128), 128)

    load_k = pltpu.make_async_copy(k_hbm, k_in, ld_sem.at[0])
    load_q = pltpu.make_async_copy(q_hbm, q_in, ld_sem.at[1])
    load_v = pltpu.make_async_copy(vm_hbm, vm, ld_sem.at[2])
    load_w = pltpu.make_async_copy(w_hbm, w_in, ld_sem.at[3])
    load_k.start()
    load_q.start()

    def suf_load(n, slot):
        return pltpu.make_async_copy(suf_hbm.at[n], sufbuf.at[slot], suf_sem.at[slot])

    barrier = pltpu.get_barrier_semaphore()

    def greet_pre(other):
        pl.semaphore_signal(barrier, inc=1, device_id={"pre": other, "head": h}, device_id_type=MESH)

    around(greet_pre)

    def greet_head(d, carry):
        pl.semaphore_signal(
            barrier, inc=1, device_id={"pre": p, "head": lax.rem(h + d, HEAD)}, device_id_type=MESH
        )
        return carry

    lax.fori_loop(1, HEAD, greet_head, 0)

    def build_t(i, carry):
        row = iota((SP, NS * NH), 0)
        col = iota((SP, NS * NH), 1)
        tmat[i] = onehot((lax.shift_right_logical(col, 4) == row) & ((col & 15) == i))
        return carry

    lax.fori_loop(0, NH, build_t, 0)
    lacc_s[...] = jnp.zeros_like(lacc_s)
    lacc[...] = jnp.zeros_like(lacc)
    pl.semaphore_wait(barrier, PRE - 1 + HEAD - 1)

    load_k.wait()

    def stage_k(i, carry):
        top = pl.multiple_of(i * 32, 32)
        mine = pl.multiple_of(i * 32 + c * 16, 16)
        for b in range(NSLOT):
            sendl[i, b] = k_in[b, pl.ds(mine, 16), lane(x)]
            sendr[i, b] = jnp.concatenate(
                [k_in[b, pl.ds(top, 16), LAT:], k_in[b, pl.ds(top + 16, 16), LAT:]], axis=-1
            )
        return carry

    lax.fori_loop(0, PRE, stage_k, 0)

    def s1l(other, src):
        return remote(sendl.at[other], krl.at[pl.ds(src * NSLOT, NSLOT)],
                      a2a_s.at[0, other], a2a_r.at[0, src], other, h)

    def s1r(other, src):
        return remote(sendr.at[other], krr.at[pl.ds(src * NSLOT, NSLOT)],
                      a2a_s.at[1, other], a2a_r.at[1, src], other, h)

    def start1(other):
        s1l(other, p).start()
        s1r(other, p).start()

    around(start1)
    krl[pl.ds(p * NSLOT, NSLOT)] = sendl[p]
    krr[pl.ds(p * NSLOT, NSLOT)] = sendr[p]

    load_q.wait()
    load_v.start()
    load_w.start()
    for n in range(NBUF):
        suf_load(n, n).start()
    q_flat = q_in[...].reshape(NS * NH, LAT + 64)
    for g in range(2):
        t_part = tmat[g * 8:(g + 1) * 8].reshape(8 * SP, NS * NH)
        q_t[g * 8:(g + 1) * 8] = nn(t_part, q_flat).astype(BF).reshape(8, SP, LAT + 64)

    def s1q(other, src):
        return remote(q_t.at[other], qr.at[src], a2a_s.at[2, other], a2a_r.at[2, src], other, h)

    around(lambda other: s1q(other, p).start())
    qr[p] = q_t[p]

    def suffix_one(n, carry):
        slot = lax.rem(n, NBUF)
        suf_load(n, slot).wait()
        qn = q_in[n]
        kn = sufbuf[slot]
        t = nt(qn, kn) * SCALE2
        t = jnp.where(iota((NH, SUF), 1) < lens[n], t, MASKED)
        m = jnp.max(t, axis=1, keepdims=True)
        w = jnp.exp2(t - m).astype(BF)
        total = jnp.sum(w.astype(F32), axis=1, keepdims=True)
        o = nn(w, kn[:, :LAT]) / total
        lat_s[pl.ds(pl.multiple_of(n * NH, NH), NH)] = o.astype(BF)
        lse = m + jnp.log2(total)
        lacc_s[...] = jnp.where(iota((NH, 128), 1) == n, lse, lacc_s[...])

        @pl.when(n + NBUF < NS)
        def _():
            suf_load(n + NBUF, slot).start()

        return carry

    lax.fori_loop(0, 8, suffix_one, 0)

    def wait1(other):
        s1l(other, other).wait_recv()
        s1r(other, other).wait_recv()

    around(wait1)

    def pick(prompt, carry):
        for b in range(8):
            slot = slots[prompt * 8 + b]
            skl[b // 4, prompt * 4 + b % 4] = krl[slot]
        for hf in range(2):
            skr[hf, prompt] = krr[slots[prompt * 8 + hf * 4 + x]]
        return carry

    lax.fori_loop(0, NPROMPT, pick, 0)

    def s2l(other, src):
        first = 5 * (other // 8) + lax.rem(other // 2, 4)
        return remote(skl.at[lax.rem(other, 2), pl.ds(first * 4, 8)], kw.at[c, :, src, :, lane(x)],
                      a2a_s.at[3, other], a2a_r.at[3, src], other, h)

    def s2r(other, src):
        first = 5 * (other // 8) + lax.rem(other // 2, 4)
        return remote(skr.at[lax.rem(other, 2), first + c], rw.at[c * 4 + x, src],
                      a2a_s.at[4, other], a2a_r.at[4, src], other, h)

    def start2(other):
        s2l(other, p).start()
        s2r(other, p).start()

    around(start2)
    own = 5 * (win // 4) + wj
    kw[c, :, p, :, lane(x)] = skl[half, pl.ds(own * 4, 8)]
    rw[c * 4 + x, p] = skr[half, own + c]

    around(lambda other: s1q(other, other).wait_recv())
    q_all = qr[...].reshape(PRE * SP, LAT + 64)
    for g in range(2):
        pick_rows = onehot(iota((320, PRE * SP), 0) + g * 320 == rank_row[...])
        sq[g * 320:(g + 1) * 320] = nn(pick_rows, q_all).astype(BF)

    def s2q(other, src):
        return remote(sq.at[pl.ds(pl.multiple_of((other // 2) * WIN, 16), WIN)], qw.at[src],
                      a2a_s.at[5, other], a2a_r.at[5, src], other, h)

    around(lambda other: s2q(other, p).start())
    qw[p] = sq[pl.ds(pl.multiple_of(win * WIN, 16), WIN)]

    lax.fori_loop(8, 14, suffix_one, 0)

    def wait2(other):
        s2l(other, other).wait_recv()
        s2r(other, other).wait_recv()

    around(wait2)

    def x_copies(d, src_x):
        to = lax.rem(x + d, 4) * 2 + c
        return (
            remote(kw.at[c, :, :, :, lane(src_x)], kw.at[c, :, :, :, lane(src_x)],
                   x_s.at[0, d - 1], x_r.at[0, d - 1], p, to),
            remote(rw.at[c * 4 + src_x], rw.at[c * 4 + src_x],
                   x_s.at[1, d - 1], x_r.at[1, d - 1], p, to),
        )

    def core_copies(d, src_x, cc):
        to = x * 2 + (1 - c)
        return (
            remote(kw.at[cc, :, :, :, lane(src_x)], kw.at[cc, :, :, :, lane(src_x)],
                   c_s.at[0, d], c_r.at[0, d], p, to),
            remote(rw.at[cc * 4 + src_x], rw.at[cc * 4 + src_x],
                   c_s.at[1, d], c_r.at[1, d], p, to),
        )

    for d in (1, 3, 2):
        for copy in x_copies(d, x):
            copy.start()
    for copy in core_copies(0, x, c):
        copy.start()

    lax.fori_loop(14, NS, suffix_one, 0)

    load_v.wait()
    for g in range(2):
        t_part = tmat[g * 8:(g + 1) * 8].reshape(8 * SP, NS * NH)
        lt_s[g * 8:(g + 1) * 8] = nn(t_part, lat_s[...]).astype(BF).reshape(8, SP, LAT)

    def project_s(i, carry):
        o_s[i] = nn(lt_s[i], vm[i]).astype(BF)
        return carry

    lax.fori_loop(0, NH, project_s, 0)
    l_s[...] = jnp.broadcast_to(lacc_s[...][:, None, :], (NH, 8, 128))

    def s4o(other, src):
        return remote(o_s.at[other], osr.at[src], a2a_s.at[6, other], a2a_r.at[6, src], other, h)

    def s4l(other, src):
        return remote(l_s.at[other], lsr.at[src], a2a_s.at[7, other], a2a_r.at[7, src], other, h)

    def start4(other):
        s4o(other, p).start()
        s4l(other, p).start()

    around(start4)
    osr[p] = o_s[p]
    lsr[p] = l_s[p]

    for d in (1, 3, 2):
        for copy in x_copies(d, lax.rem(x + 4 - d, 4)):
            copy.wait_recv()
        for copy in core_copies(d, lax.rem(x + 4 - d, 4), c):
            copy.start()

    around(lambda other: s2q(other, other).wait_recv())
    for d in (0, 1, 3, 2):
        for copy in core_copies(d, lax.rem(x + 4 - d, 4), 1 - c):
            copy.wait_recv()

    def chunk(t, carry):
        rows = pl.ds(pl.multiple_of(t * 16, 16), 16)
        ab = (t + wj) // 4
        ql = qw[:, rows, :LAT].reshape(256, LAT)
        qrope = qw[:, rows, LAT:].reshape(256, 64)
        none = jnp.zeros_like(qrope)
        q_side = (jnp.concatenate([qrope, none], axis=-1), jnp.concatenate([none, qrope], axis=-1))
        rope = rw[pl.ds(ab * 4, 4)].reshape(1024, 128)
        scores = []
        for cc in range(2):
            keys = kw[cc, pl.ds(ab * 4, 4)].reshape(1024, LAT)
            scores.append((nt(ql, keys) + nt(q_side[cc], rope)) * SCALE2)
        m = jnp.maximum(
            jnp.max(scores[0], axis=1, keepdims=True), jnp.max(scores[1], axis=1, keepdims=True)
        )
        total = jnp.zeros((256, 1), F32)
        acc = jnp.zeros((256, LAT), F32)
        for cc in range(2):
            w = jnp.exp2(scores[cc] - m).astype(BF)
            total = total + jnp.sum(w.astype(F32), axis=1, keepdims=True)
            acc = acc + nn(w, kw[cc, pl.ds(ab * 4, 4)].reshape(1024, LAT))
        ol[:, rows] = (acc / total).astype(BF).reshape(NH, 16, LAT)
        lse = (m + jnp.log2(total)).reshape(NH, 16, 1)
        here = iota((NH, 16, 128), 2) == iota((NH, 16, 128), 1) + t * 16
        lacc[...] += jnp.sum(jnp.where(here, lse, 0.0), axis=1)
        return carry

    lax.fori_loop(0, WIN // 16, chunk, 0)
    lps[...] = jnp.broadcast_to(lacc[...][:, None, :], (NH, 8, 128))

    def s5o(other, src):
        return remote(op.at[other], orr.at[src // 2, :, lane(lax.rem(src, 2))],
                      a2a_s.at[8, other], a2a_r.at[8, src], other, h)

    def s5l(other, src):
        return remote(lps.at[other], lr.at[src], a2a_s.at[9, other], a2a_r.at[9, src], other, h)

    def start5(other):
        op[other] = nn(ol[other], vm[other]).astype(BF)
        s5o(other, p).start()
        s5l(other, p).start()

    around(start5)
    orr[win, :, lane(half)] = nn(ol[p], vm[p]).astype(BF)
    lr[p] = lps[p]

    def wait4(other):
        s4o(other, other).wait_recv()
        s4l(other, other).wait_recv()

    around(wait4)

    def spread(src, carry):
        rows = pl.ds(pl.multiple_of(src * NS, 8), NS)
        suf_o[rows] = osr[src].astype(F32)[:NS]
        row = jnp.broadcast_to(lsr[src][0:1], (NS, 128))
        col = jnp.sum(jnp.where(iota((NS, 128), 0) == iota((NS, 128), 1), row, 0.0), axis=1, keepdims=True)
        suf_l[rows] = jnp.broadcast_to(col, (NS, 128))
        return carry

    lax.fori_loop(0, PRE, spread, 0)

    def wait5(other):
        s5o(other, other).wait_recv()
        s5l(other, other).wait_recv()

    around(wait5)

    def merge(g, carry):
        rows = pl.ds(pl.multiple_of(g * 320, 64), 320)
        rank = rank_col[rows]
        pick_rows = onehot(iota((320, PRE * NS), 1) == rank)
        parts = nn(pick_rows, orr[...].reshape(PRE * NS, 2 * VD))
        at = iota((320, 128), 1)
        la = jnp.zeros((320, 128), F32)
        lb = jnp.zeros((320, 128), F32)
        for w in range(8):
            hit = (at == rank - w * WIN) & (at < WIN)
            la = la + jnp.where(hit, lr[2 * w][0:1], 0.0)
            lb = lb + jnp.where(hit, lr[2 * w + 1][0:1], 0.0)
        la = jnp.sum(la, axis=1, keepdims=True)
        lb = jnp.sum(lb, axis=1, keepdims=True)
        ls = suf_l[rows]
        top = jnp.maximum(jnp.maximum(la, lb), ls)
        ea, eb, es = jnp.exp2(la - top), jnp.exp2(lb - top), jnp.exp2(ls - top)
        merged = (ea * parts[:, :VD] + eb * parts[:, VD:] + es * suf_o[rows]) / (ea + eb + es)
        hbuf[rows, lane(p)] = merged.astype(BF)
        return carry

    lax.fori_loop(0, 2, merge, 0)

    def g_copy(rows, piece, dy, dz, ssem, rsem):
        view = hbuf.at[pl.ds(rows * 320, 320), lane(piece)]
        return remote(view, view, ssem, rsem, lax.rem(y + dy, 4) * 4 + lax.rem(z + dz, 4), h)

    def piece_of(by, bz):
        return lax.rem(y + 4 - by, 4) * 4 + lax.rem(z + 4 - bz, 4)

    def first(rows, d, piece):
        dy, dz = (0, d) if rows == 0 else (d, 0)
        return g_copy(rows, piece, dy, dz, g1_s.at[rows, d - 1], g1_r.at[rows, d - 1])

    def second(rows, k, d, piece):
        dy, dz = (d, 0) if rows == 0 else (0, d)
        return g_copy(rows, piece, dy, dz, g2_s.at[rows, k * 3 + d - 1], g2_r.at[rows, k * 3 + d - 1])

    for d in (1, 3, 2):
        for rows in range(2):
            first(rows, d, p).start()
    for d in (1, 3, 2):
        for rows in range(2):
            second(rows, 0, d, p).start()
    for k in (1, 3, 2):
        for rows in range(2):
            got = piece_of(0, k) if rows == 0 else piece_of(k, 0)
            first(rows, k, got).wait_recv()
            for d in (1, 3, 2):
                second(rows, k, d, got).start()
    for k in (0, 1, 3, 2):
        for d in (1, 3, 2):
            for rows in range(2):
                got = piece_of(d, k) if rows == 0 else piece_of(k, d)
                second(rows, k, d, got).wait_recv()

    load_w.wait()

    def out_rows(g, carry):
        rows = pl.ds(pl.multiple_of(g * 320, 64), 320)
        pb[pl.ds(g * 4, 4)] = nn(hbuf[rows], w_in[...]).astype(BF).reshape(4, WIN, 448)
        return carry

    lax.fori_loop(0, 2, out_rows, 0)

    def s6(other, src):
        return remote(pb.at[other], rs.at[src], e_s.at[other], e_r.at[src], p, other)

    def heads(fn):
        def body(d, carry):
            fn(lax.rem(h + d, HEAD))
            return carry
        lax.fori_loop(1, HEAD, body, 0)

    heads(lambda other: s6(other, h).start())
    rs[h] = pb[h]
    heads(lambda other: s6(other, other).wait_recv())
    total = rs[0].astype(F32)
    for k in range(1, HEAD):
        total = total + rs[k].astype(F32)
    out[...] = total.astype(BF)

    def sent(other):
        for copy in (s1l, s1r, s1q, s2l, s2r, s2q, s4o, s4l, s5o, s5l):
            copy(other, p).wait_send()

    around(sent)
    for d in (1, 2, 3):
        for copy in x_copies(d, x):
            copy.wait_send()
    for d in range(4):
        for copy in core_copies(d, lax.rem(x + 4 - d, 4), c):
            copy.wait_send()
    for rows in range(2):
        for d in (1, 2, 3):
            first(rows, d, p).wait_send()
        for k in range(4):
            for d in (1, 2, 3):
                second(rows, k, d, p).wait_send()
    heads(lambda other: s6(other, h).wait_send())


def per_device(
    query_latent, prefix_cache, block_slot, sample_prompt, suffix_cache, suffix_length, value_map, out_weight
):
    sp = sample_prompt
    n = jnp.arange(sp.shape[0], dtype=jnp.int32)
    earlier = (sp[None, :] == sp[:, None]) & (n[None, :] < n[:, None])
    rank = sp * GROUP + jnp.sum(earlier.astype(jnp.int32), axis=1)
    rank_row = jnp.pad(rank.reshape(PRE, NS), ((0, 0), (0, SP - NS)), constant_values=-1).reshape(1, PRE * SP)
    rank_col = rank.reshape(-1, 1)
    vmem = pl.BlockSpec(memory_space=pltpu.VMEM)
    smem = pl.BlockSpec(memory_space=pltpu.SMEM)
    hbm = pl.BlockSpec(memory_space=pl.ANY)
    V = pltpu.VMEM
    dma = pltpu.SemaphoreType.DMA
    width = LAT + 64
    scratch = [
        V((NS, NH, width), BF), V((NSLOT, 512, width), BF), V((NH, LAT, VD), BF), V((NH * VD, 448), BF),
        V((NBUF, SUF, width), BF),
        V((NH, SP, NS * NH), BF), V((NH, SP, width), BF), V((PRE, SP, width), BF),
        V((PRE, NSLOT, 16, 128), BF), V((PRE, NSLOT, 16, 128), BF),
        V((PRE * NSLOT, 16, 128), BF), V((PRE * NSLOT, 16, 128), BF),
        V((2, NPROMPT * 4, 16, 128), BF), V((2, NPROMPT, 16, 128), BF),
        V((PRE * NS, width), BF), V((NH, WIN, width), BF),
        V((2, 8, PRE, 16, LAT), BF), V((8, PRE, 16, 128), BF),
        V((NS * NH, LAT), BF), V((NH, SP, LAT), BF), V((NH, SP, VD), BF), V((NH, 8, 128), F32),
        V((PRE, SP, VD), BF), V((PRE, 8, 128), F32), V((NH, 128), F32),
        V((NH, WIN, LAT), BF), V((NH, WIN, VD), BF), V((NH, 8, 128), F32),
        V((8, WIN, 2 * VD), BF), V((PRE, 8, 128), F32), V((NH, 128), F32),
        V((PRE * NS, VD), F32), V((PRE * NS, 128), F32), V((PRE * NS, NH * VD), BF),
        V((HEAD, WIN, 448), BF), V((HEAD, WIN, 448), BF),
        dma((4,)), dma((NBUF,)), dma((10, PRE)), dma((10, PRE)),
        dma((2, 3)), dma((2, 3)), dma((2, 4)), dma((2, 4)),
        dma((2, 3)), dma((2, 3)), dma((2, 12)), dma((2, 12)), dma((HEAD,)), dma((HEAD,)),
    ]
    return pl.pallas_call(
        kernel,
        out_shape=jax.ShapeDtypeStruct((WIN, 448), BF),
        in_specs=[hbm, hbm, hbm, hbm, hbm, vmem, vmem, smem, smem],
        out_specs=vmem,
        scratch_shapes=scratch,
        compiler_params=pltpu.CompilerParams(
            collective_id=0, has_side_effects=True, vmem_limit_bytes=58 * 1024 * 1024
        ),
        cost_estimate=pl.CostEstimate(flops=10_000_000_000, bytes_accessed=30_000_000, transcendentals=3_000_000),
    )(
        query_latent, prefix_cache, suffix_cache, value_map, out_weight,
        rank_row, rank_col, block_slot.reshape(-1), suffix_length,
    )


def solution(mesh):
    return jax.shard_map(
        per_device,
        mesh=mesh,
        in_specs=(
            P("pre", "head", None),
            P("pre", None, None),
            P(),
            P(),
            P("pre", None, None),
            P("pre"),
            P("head", None, None),
            P("head", "pre"),
        ),
        out_specs=P("head", "pre"),
        check_vma=False,
    )
```

```python
import functools
import math

import jax
import jax.numpy as jnp
from jax import lax
from jax.experimental import pallas as pl
from jax.experimental.pallas import tpu as pltpu
from jax.sharding import PartitionSpec as P

GROUP = 64
PRE = 16
HEAD = 8
NS = 40
SP = 48
NH = 16
LAT = 512
VD = 128
SUF = 384
WIN = 80
NSLOT = 5
NPROMPT = 10
NBUF = 4
MASKED = -1e30
SCALE2 = math.log2(math.e) / math.sqrt(192.0)

BF = jnp.bfloat16
F32 = jnp.float32
MESH = pl.DeviceIdType.MESH


def nt(a, b):
    return lax.dot_general(a, b, (((1,), (1,)), ((), ())), preferred_element_type=F32)


def nn(a, b):
    return lax.dot_general(a, b, (((1,), (0,)), ((), ())), preferred_element_type=F32)


def onehot(mask):
    return jnp.where(mask, 1.0, 0.0).astype(BF)


def iota(shape, dim):
    return lax.broadcasted_iota(jnp.int32, shape, dim)


def kernel(
    q_hbm, k_hbm, suf_hbm, vm_hbm, w_hbm, prompt_row, slots, lens,
    out,
    q_in, vm, w_in, sufbuf,
    tmat, q_t, qr, krl, krr,
    skl, skr, sq, qw, kw, rank_row, rank_col,
    lat_s, lt_s, o_s, l_s, osr, lsr, lacc_s,
    ol, op, lps, orr, lr, lacc,
    suf_o, suf_l, hbuf, pb, rs,
    ld_sem, suf_sem, a2a_s, a2a_r, x_s, x_r, c_s, c_r, g1_s, g1_r, g2_s, g2_r, e_s, e_r,
):
    p = lax.axis_index("pre")
    h = lax.axis_index("head")
    x, c = h // 2, lax.rem(h, 2)
    y, z = p // 4, lax.rem(p, 4)
    win, half = p // 2, lax.rem(p, 2)
    wj = lax.rem(win, 4)

    def remote(src, dst, ssem, rsem, pre, head):
        return pltpu.make_async_remote_copy(
            src_ref=src, dst_ref=dst, send_sem=ssem, recv_sem=rsem,
            device_id={"pre": pre, "head": head}, device_id_type=MESH,
        )

    def around(fn):
        def body(d, carry):
            fn(lax.rem(p + d, PRE))
            return carry
        lax.fori_loop(1, PRE, body, 0)

    def lane(i):
        return pl.ds(pl.multiple_of(i * 128, 128), 128)

    load_q = pltpu.make_async_copy(q_hbm, q_in, ld_sem.at[4])
    load_v = pltpu.make_async_copy(vm_hbm, vm, ld_sem.at[2])
    load_w = pltpu.make_async_copy(w_hbm, w_in, ld_sem.at[3])
    load_q.start()

    def suf_load(n, slot):
        return pltpu.make_async_copy(suf_hbm.at[n], sufbuf.at[slot], suf_sem.at[slot])

    barrier = pltpu.get_barrier_semaphore()

    def greet_pre(other):
        pl.semaphore_signal(barrier, inc=1, device_id={"pre": other, "head": h}, device_id_type=MESH)

    around(greet_pre)

    def greet_head(d, carry):
        pl.semaphore_signal(
            barrier, inc=1, device_id={"pre": p, "head": lax.rem(h + d, HEAD)}, device_id_type=MESH
        )
        return carry

    lax.fori_loop(1, HEAD, greet_head, 0)

    def build_t(i, carry):
        row = iota((SP, NS * NH), 0)
        col = iota((SP, NS * NH), 1)
        tmat[i] = onehot((lax.shift_right_logical(col, 4) == row) & ((col & 15) == i))
        return carry

    lax.fori_loop(0, NH, build_t, 0)

    names = jnp.broadcast_to(prompt_row[...], (SP, PRE * SP))
    at = iota((SP, PRE * SP), 1)
    rank_row[...] = prompt_row[...] * GROUP

    def build_rank(i, carry):
        ids = iota((SP, PRE * SP), 0) + i * SP
        name = jnp.sum(jnp.where(at == ids, names, 0), axis=1, keepdims=True)
        same = names == name
        before = jnp.sum(jnp.where(same & (at < ids), 1, 0), axis=1, keepdims=True)
        rank_col[pl.ds(pl.multiple_of(i * NS, 8), NS)] = (name * GROUP + before)[:NS]
        rank_row[...] += jnp.sum(jnp.where(same & (ids < at), 1, 0), axis=0, keepdims=True)
        return carry

    lax.fori_loop(0, PRE, build_rank, 0)
    lacc_s[...] = jnp.zeros_like(lacc_s)
    lacc[...] = jnp.zeros_like(lacc)
    pl.semaphore_wait(barrier, PRE - 1 + HEAD - 1)

    def tiles(i):
        return (
            k_hbm.at[:, pl.ds(pl.multiple_of(c * 256 + i * 16, 16), 16), lane(x)],
            k_hbm.at[:, pl.ds(pl.multiple_of(LAT + lax.rem(i, 4) * 16, 16), 16), lane(x)],
        )

    def s1l(other, src):
        return remote(tiles(other)[0], krl.at[pl.ds(src * NSLOT, NSLOT)],
                      a2a_s.at[0, other], a2a_r.at[0, src], other, h)

    def s1r(other, src):
        return remote(tiles(other)[1], krr.at[pl.ds(src * NSLOT, NSLOT)],
                      a2a_s.at[1, other], a2a_r.at[1, src], other, h)

    def start1(other):
        s1l(other, p).start()
        s1r(other, p).start()

    around(start1)
    own_l = pltpu.make_async_copy(tiles(p)[0], krl.at[pl.ds(p * NSLOT, NSLOT)], ld_sem.at[0])
    own_r = pltpu.make_async_copy(tiles(p)[1], krr.at[pl.ds(p * NSLOT, NSLOT)], ld_sem.at[1])
    own_l.start()
    own_r.start()

    load_q.wait()
    load_v.start()
    load_w.start()
    for n in range(NBUF):
        suf_load(n, n).start()
    q_flat = q_in[...].reshape(NS * NH, LAT + 64)
    for g in range(2):
        t_part = tmat[g * 8:(g + 1) * 8].reshape(8 * SP, NS * NH)
        q_t[g * 8:(g + 1) * 8] = nn(t_part, q_flat).astype(BF).reshape(8, SP, LAT + 64)

    def s1q(other, src):
        return remote(q_t.at[other], qr.at[src], a2a_s.at[2, other], a2a_r.at[2, src], other, h)

    around(lambda other: s1q(other, p).start())
    qr[p] = q_t[p]

    def suffix_one(n, carry):
        slot = lax.rem(n, NBUF)
        suf_load(n, slot).wait()
        qn = q_in[n]
        kn = sufbuf[slot]
        t = nn(qn, kn) * SCALE2
        t = jnp.where(iota((NH, SUF), 1) < lens[n], t, MASKED)
        m = jnp.max(t, axis=1, keepdims=True)
        w = jnp.exp2(t - m).astype(BF)
        total = jnp.sum(w.astype(F32), axis=1, keepdims=True)
        o = nt(w, kn[:LAT]) / total
        lat_s[pl.ds(pl.multiple_of(n * NH, NH), NH)] = o.astype(BF)
        lse = m + jnp.log2(total)
        lacc_s[...] = jnp.where(iota((NH, 128), 1) == n, lse, lacc_s[...])

        @pl.when(n + NBUF < NS)
        def _():
            suf_load(n + NBUF, slot).start()

        return carry

    lax.fori_loop(0, 8, suffix_one, 0)

    def wait1(other):
        s1l(other, other).wait_recv()
        s1r(other, other).wait_recv()

    around(wait1)
    own_l.wait()
    own_r.wait()

    def pick(prompt, carry):
        for b in range(8):
            slot = slots[b, prompt]
            skl[b // 4, prompt * 4 + b % 4] = krl[slot]
        for hf in range(2):
            skr[hf, prompt] = krr[slots[hf * 4 + p // 4, prompt]]
        return carry

    lax.fori_loop(0, NPROMPT, pick, 0)

    def s2l(other, src):
        first = 5 * (other // 8) + lax.rem(other // 2, 4)
        rows = pl.ds(pl.multiple_of(c * 256 + src * 16, 16), 16)
        return remote(skl.at[lax.rem(other, 2), pl.ds(first * 4, 8)], kw.at[:, rows, lane(x)],
                      a2a_s.at[3, other], a2a_r.at[3, src], other, h)

    def s2r(other, src):
        first = 5 * (other // 8) + lax.rem(other // 2, 4)
        rows = pl.ds(pl.multiple_of(LAT + lax.rem(src, 4) * 16, 16), 16)
        return remote(skr.at[lax.rem(other, 2), first + c], kw.at[c * 4 + src // 4, rows, lane(x)],
                      a2a_s.at[4, other], a2a_r.at[4, src], other, h)

    def start2(other):
        s2l(other, p).start()
        s2r(other, p).start()

    around(start2)
    own = 5 * (win // 4) + wj
    kw[:, pl.ds(pl.multiple_of(c * 256 + p * 16, 16), 16), lane(x)] = skl[half, pl.ds(own * 4, 8)]
    kw[c * 4 + p // 4, pl.ds(pl.multiple_of(LAT + lax.rem(p, 4) * 16, 16), 16), lane(x)] = skr[half, own + c]

    around(lambda other: s1q(other, other).wait_recv())
    q_all = qr[...].reshape(PRE * SP, LAT + 64)
    for g in range(2):
        pick_rows = onehot(iota((320, PRE * SP), 0) + g * 320 == rank_row[...])
        sq[g * 320:(g + 1) * 320] = nn(pick_rows, q_all).astype(BF)

    def s2q(other, src):
        return remote(sq.at[pl.ds(pl.multiple_of((other // 2) * WIN, 16), WIN)], qw.at[src],
                      a2a_s.at[5, other], a2a_r.at[5, src], other, h)

    around(lambda other: s2q(other, p).start())
    qw[p] = sq[pl.ds(pl.multiple_of(win * WIN, 16), WIN)]

    lax.fori_loop(8, 14, suffix_one, 0)

    def wait2(other):
        s2l(other, other).wait_recv()
        s2r(other, other).wait_recv()

    around(wait2)

    def part(cc, src_x):
        rows = pl.ds(pl.multiple_of(cc * 256, 256), 256)
        return kw.at[:, rows, lane(src_x)], kw.at[pl.ds(cc * 4, 4), LAT:, lane(src_x)]

    def x_copies(d, src_x):
        to = lax.rem(x + d, 4) * 2 + c
        return [
            remote(view, view, x_s.at[k, d - 1], x_r.at[k, d - 1], p, to)
            for k, view in enumerate(part(c, src_x))
        ]

    def core_copies(d, src_x, cc):
        to = x * 2 + (1 - c)
        return [
            remote(view, view, c_s.at[k, d], c_r.at[k, d], p, to)
            for k, view in enumerate(part(cc, src_x))
        ]

    for d in (1, 3, 2):
        for copy in x_copies(d, x):
            copy.start()
    for copy in core_copies(0, x, c):
        copy.start()

    lax.fori_loop(14, NS, suffix_one, 0)

    load_v.wait()
    for g in range(2):
        t_part = tmat[g * 8:(g + 1) * 8].reshape(8 * SP, NS * NH)
        lt_s[g * 8:(g + 1) * 8] = nn(t_part, lat_s[...]).astype(BF).reshape(8, SP, LAT)

    def project_s(i, carry):
        o_s[i] = nn(lt_s[i], vm[i]).astype(BF)
        return carry

    lax.fori_loop(0, NH, project_s, 0)
    l_s[...] = jnp.broadcast_to(lacc_s[...][:, None, :], (NH, 8, 128))

    def s4o(other, src):
        return remote(o_s.at[other], osr.at[src], a2a_s.at[6, other], a2a_r.at[6, src], other, h)

    def s4l(other, src):
        return remote(l_s.at[other], lsr.at[src], a2a_s.at[7, other], a2a_r.at[7, src], other, h)

    def start4(other):
        s4o(other, p).start()
        s4l(other, p).start()

    around(start4)
    osr[p] = o_s[p]
    lsr[p] = l_s[p]

    for d in (1, 3, 2):
        for copy in x_copies(d, lax.rem(x + 4 - d, 4)):
            copy.wait_recv()
        for copy in core_copies(d, lax.rem(x + 4 - d, 4), c):
            copy.start()

    around(lambda other: s2q(other, other).wait_recv())
    for d in (0, 1, 3, 2):
        for copy in core_copies(d, lax.rem(x + 4 - d, 4), 1 - c):
            copy.wait_recv()

    def chunk(t, carry):
        rows = pl.ds(pl.multiple_of(t * 16, 16), 16)
        ab = (t + wj) // 4
        qc = qw[:, rows].reshape(256, LAT + 64)
        scores = [nn(qc, kw[ab * 4 + b]) * SCALE2 for b in range(4)]
        m = functools.reduce(jnp.maximum, [jnp.max(t, axis=1, keepdims=True) for t in scores])
        total = jnp.zeros((256, 1), F32)
        acc = jnp.zeros((256, LAT), F32)
        for b in range(4):
            w = jnp.exp2(scores[b] - m).astype(BF)
            total = total + jnp.sum(w.astype(F32), axis=1, keepdims=True)
            acc = acc + nt(w, kw[ab * 4 + b, :LAT])
        ol[:, rows] = (acc / total).astype(BF).reshape(NH, 16, LAT)
        lse = (m + jnp.log2(total)).reshape(NH, 16, 1)
        here = iota((NH, 16, 128), 2) == iota((NH, 16, 128), 1) + t * 16
        lacc[...] += jnp.sum(jnp.where(here, lse, 0.0), axis=1)
        return carry

    lax.fori_loop(0, WIN // 16, chunk, 0)
    lps[...] = jnp.broadcast_to(lacc[...][:, None, :], (NH, 8, 128))

    def s5o(other, src):
        return remote(op.at[other], orr.at[src // 2, :, lane(lax.rem(src, 2))],
                      a2a_s.at[8, other], a2a_r.at[8, src], other, h)

    def s5l(other, src):
        return remote(lps.at[other], lr.at[src], a2a_s.at[9, other], a2a_r.at[9, src], other, h)

    def start5(other):
        op[other] = nn(ol[other], vm[other]).astype(BF)
        s5o(other, p).start()
        s5l(other, p).start()

    around(start5)
    orr[win, :, lane(half)] = nn(ol[p], vm[p]).astype(BF)
    lr[p] = lps[p]

    def wait4(other):
        s4o(other, other).wait_recv()
        s4l(other, other).wait_recv()

    around(wait4)

    def spread(src, carry):
        rows = pl.ds(pl.multiple_of(src * NS, 8), NS)
        suf_o[rows] = osr[src].astype(F32)[:NS]
        row = jnp.broadcast_to(lsr[src][0:1], (NS, 128))
        col = jnp.sum(jnp.where(iota((NS, 128), 0) == iota((NS, 128), 1), row, 0.0), axis=1, keepdims=True)
        suf_l[rows] = jnp.broadcast_to(col, (NS, 128))
        return carry

    lax.fori_loop(0, PRE, spread, 0)

    def wait5(other):
        s5o(other, other).wait_recv()
        s5l(other, other).wait_recv()

    around(wait5)

    def merge(g, carry):
        rows = pl.ds(pl.multiple_of(g * 320, 64), 320)
        rank = rank_col[rows]
        pick_rows = onehot(iota((320, PRE * NS), 1) == rank)
        parts = nn(pick_rows, orr[...].reshape(PRE * NS, 2 * VD))
        at = iota((320, 128), 1)
        la = jnp.zeros((320, 128), F32)
        lb = jnp.zeros((320, 128), F32)
        for w in range(8):
            hit = (at == rank - w * WIN) & (at < WIN)
            la = la + jnp.where(hit, lr[2 * w][0:1], 0.0)
            lb = lb + jnp.where(hit, lr[2 * w + 1][0:1], 0.0)
        la = jnp.sum(la, axis=1, keepdims=True)
        lb = jnp.sum(lb, axis=1, keepdims=True)
        ls = suf_l[rows]
        top = jnp.maximum(jnp.maximum(la, lb), ls)
        ea, eb, es = jnp.exp2(la - top), jnp.exp2(lb - top), jnp.exp2(ls - top)
        merged = (ea * parts[:, :VD] + eb * parts[:, VD:] + es * suf_o[rows]) / (ea + eb + es)
        hbuf[rows, lane(p)] = merged.astype(BF)
        return carry

    lax.fori_loop(0, 2, merge, 0)

    def g_copy(rows, piece, dy, dz, ssem, rsem):
        view = hbuf.at[pl.ds(rows * 320, 320), lane(piece)]
        return remote(view, view, ssem, rsem, lax.rem(y + dy, 4) * 4 + lax.rem(z + dz, 4), h)

    def piece_of(by, bz):
        return lax.rem(y + 4 - by, 4) * 4 + lax.rem(z + 4 - bz, 4)

    def first(rows, d, piece):
        dy, dz = (0, d) if rows == 0 else (d, 0)
        return g_copy(rows, piece, dy, dz, g1_s.at[rows, d - 1], g1_r.at[rows, d - 1])

    def second(rows, k, d, piece):
        dy, dz = (d, 0) if rows == 0 else (0, d)
        return g_copy(rows, piece, dy, dz, g2_s.at[rows, k * 3 + d - 1], g2_r.at[rows, k * 3 + d - 1])

    for d in (1, 3, 2):
        for rows in range(2):
            first(rows, d, p).start()
    for d in (1, 3, 2):
        for rows in range(2):
            second(rows, 0, d, p).start()
    for k in (1, 3, 2):
        for rows in range(2):
            got = piece_of(0, k) if rows == 0 else piece_of(k, 0)
            first(rows, k, got).wait_recv()
            for d in (1, 3, 2):
                second(rows, k, d, got).start()
    for k in (0, 1, 3, 2):
        for d in (1, 3, 2):
            for rows in range(2):
                got = piece_of(d, k) if rows == 0 else piece_of(k, d)
                second(rows, k, d, got).wait_recv()

    load_w.wait()

    def out_rows(g, carry):
        rows = pl.ds(pl.multiple_of(g * 320, 64), 320)
        pb[pl.ds(g * 4, 4)] = nt(hbuf[rows], w_in[...]).astype(BF).reshape(4, WIN, 448)
        return carry

    lax.fori_loop(0, 2, out_rows, 0)

    def s6(other, src):
        return remote(pb.at[other], rs.at[src], e_s.at[other], e_r.at[src], p, other)

    def heads(fn):
        def body(d, carry):
            fn(lax.rem(h + d, HEAD))
            return carry
        lax.fori_loop(1, HEAD, body, 0)

    heads(lambda other: s6(other, h).start())
    rs[h] = pb[h]
    heads(lambda other: s6(other, other).wait_recv())
    total = rs[0].astype(F32)
    for k in range(1, HEAD):
        total = total + rs[k].astype(F32)
    out[...] = total.astype(BF)

    def sent(other):
        for copy in (s1l, s1r, s1q, s2l, s2r, s2q, s4o, s4l, s5o, s5l):
            copy(other, p).wait_send()

    around(sent)
    for d in (1, 2, 3):
        for copy in x_copies(d, x):
            copy.wait_send()
    for d in range(4):
        for copy in core_copies(d, lax.rem(x + 4 - d, 4), c):
            copy.wait_send()
    for rows in range(2):
        for d in (1, 2, 3):
            first(rows, d, p).wait_send()
        for k in range(4):
            for d in (1, 2, 3):
                second(rows, k, d, p).wait_send()
    heads(lambda other: s6(other, h).wait_send())


def per_device(
    query_latent, prefix_cache, block_slot, sample_prompt, suffix_cache, suffix_length, value_map, out_weight
):
    prompt_row = jnp.pad(
        sample_prompt.reshape(PRE, NS), ((0, 0), (0, SP - NS)), constant_values=-4
    ).reshape(1, PRE * SP)
    vmem = pl.BlockSpec(memory_space=pltpu.VMEM)
    smem = pl.BlockSpec(memory_space=pltpu.SMEM)
    hbm = pl.BlockSpec(memory_space=pl.ANY)
    V = pltpu.VMEM
    dma = pltpu.SemaphoreType.DMA
    width = LAT + 64
    scratch = [
        V((NS, NH, width), BF), V((NH, LAT, VD), BF), V((448, NH * VD), BF),
        V((NBUF, width, SUF), BF),
        V((NH, SP, NS * NH), BF), V((NH, SP, width), BF), V((PRE, SP, width), BF),
        V((PRE * NSLOT, 16, 128), BF), V((PRE * NSLOT, 16, 128), BF),
        V((2, NPROMPT * 4, 16, 128), BF), V((2, NPROMPT, 16, 128), BF),
        V((PRE * NS, width), BF), V((NH, WIN, width), BF),
        V((8, width, 512), BF), V((1, PRE * SP), jnp.int32), V((PRE * NS, 1), jnp.int32),
        V((NS * NH, LAT), BF), V((NH, SP, LAT), BF), V((NH, SP, VD), BF), V((NH, 8, 128), F32),
        V((PRE, SP, VD), BF), V((PRE, 8, 128), F32), V((NH, 128), F32),
        V((NH, WIN, LAT), BF), V((NH, WIN, VD), BF), V((NH, 8, 128), F32),
        V((8, WIN, 2 * VD), BF), V((PRE, 8, 128), F32), V((NH, 128), F32),
        V((PRE * NS, VD), F32), V((PRE * NS, 128), F32), V((PRE * NS, NH * VD), BF),
        V((HEAD, WIN, 448), BF), V((HEAD, WIN, 448), BF),
        dma((5,)), dma((NBUF,)), dma((10, PRE)), dma((10, PRE)),
        dma((2, 3)), dma((2, 3)), dma((2, 4)), dma((2, 4)),
        dma((2, 3)), dma((2, 3)), dma((2, 12)), dma((2, 12)), dma((HEAD,)), dma((HEAD,)),
    ]
    return pl.pallas_call(
        kernel,
        out_shape=jax.ShapeDtypeStruct((WIN, 448), BF),
        in_specs=[hbm, hbm, hbm, hbm, hbm, vmem, smem, smem],
        out_specs=vmem,
        scratch_shapes=scratch,
        compiler_params=pltpu.CompilerParams(
            collective_id=0, has_side_effects=True, vmem_limit_bytes=58 * 1024 * 1024
        ),
        cost_estimate=pl.CostEstimate(flops=10_000_000_000, bytes_accessed=30_000_000, transcendentals=3_000_000),
    )(
        query_latent, prefix_cache.transpose(0, 2, 1), suffix_cache.transpose(0, 2, 1), value_map, out_weight.T,
        prompt_row, block_slot.T, suffix_length,
    )


def solution(mesh):
    return jax.shard_map(
        per_device,
        mesh=mesh,
        in_specs=(
            P("pre", "head", None),
            P("pre", None, None),
            P(),
            P(),
            P("pre", None, None),
            P("pre"),
            P("head", None, None),
            P("head", "pre"),
        ),
        out_specs=P("head", "pre"),
        check_vma=False,
    )
```

```python
import functools
import math

import jax
import jax.numpy as jnp
from jax import lax
from jax.experimental import pallas as pl
from jax.experimental.pallas import tpu as pltpu
from jax.sharding import PartitionSpec as P

GROUP = 64
PRE = 16
HEAD = 8
NS = 40
SP = 48
NH = 16
LAT = 512
VD = 128
SUF = 384
WIN = 80
NSLOT = 5
NPROMPT = 10
NBUF = 4
MASKED = -1e30
GROUPS = ((0, 16, 0), (16, 32, 128), (48, 32, 384))
SCALE2 = math.log2(math.e) / math.sqrt(192.0)

BF = jnp.bfloat16
F32 = jnp.float32
MESH = pl.DeviceIdType.MESH


def nt(a, b):
    return lax.dot_general(a, b, (((1,), (1,)), ((), ())), preferred_element_type=F32)


def nn(a, b):
    return lax.dot_general(a, b, (((1,), (0,)), ((), ())), preferred_element_type=F32)


def onehot(mask):
    return jnp.where(mask, 1.0, 0.0).astype(BF)


def iota(shape, dim):
    return lax.broadcasted_iota(jnp.int32, shape, dim)


def kernel(
    q_hbm, k_hbm, suf_hbm, vm_hbm, w_hbm, prompt_row, slots, lens,
    out,
    q_in, vm, w_in, sufbuf,
    tmat, q_t, qr, krl, krr,
    skl, skr, sq, qw, kw, rank_row, rank_col, sort, unsort,
    lat_s, lt_s, o_s, l_s, osr, lsr, lacc_s,
    ol, op, lps, orr, lr, lacc,
    suf_rhs, suf, hbuf, part_o, pb, rs,
    ld_sem, suf_sem, a2a_s, a2a_r, x_s, x_r, c_s, c_r, g1_s, g1_r, g2_s, g2_r, e_s, e_r,
):
    p = lax.axis_index("pre")
    h = lax.axis_index("head")
    x, c = h // 2, lax.rem(h, 2)
    y, z = p // 4, lax.rem(p, 4)
    win, half = p // 2, lax.rem(p, 2)
    wj = lax.rem(win, 4)

    def remote(src, dst, ssem, rsem, pre, head):
        return pltpu.make_async_remote_copy(
            src_ref=src, dst_ref=dst, send_sem=ssem, recv_sem=rsem,
            device_id={"pre": pre, "head": head}, device_id_type=MESH,
        )

    def around(fn):
        def body(d, carry):
            fn(lax.rem(p + d, PRE))
            return carry
        lax.fori_loop(1, PRE, body, 0)

    def lane(i):
        return pl.ds(pl.multiple_of(i * 128, 128), 128)

    load_q = pltpu.make_async_copy(q_hbm, q_in, ld_sem.at[4])
    load_v = pltpu.make_async_copy(vm_hbm, vm, ld_sem.at[2])
    load_w = pltpu.make_async_copy(w_hbm, w_in, ld_sem.at[3])
    load_q.start()

    def suf_load(n, slot):
        return pltpu.make_async_copy(suf_hbm.at[n], sufbuf.at[slot], suf_sem.at[slot])

    barrier = pltpu.get_barrier_semaphore()

    def greet_pre(other):
        pl.semaphore_signal(barrier, inc=1, device_id={"pre": other, "head": h}, device_id_type=MESH)

    around(greet_pre)

    def greet_head(d, carry):
        pl.semaphore_signal(
            barrier, inc=1, device_id={"pre": p, "head": lax.rem(h + d, HEAD)}, device_id_type=MESH
        )
        return carry

    lax.fori_loop(1, HEAD, greet_head, 0)

    def build_t(i, carry):
        row = iota((SP, NS * NH), 0)
        col = iota((SP, NS * NH), 1)
        tmat[i] = onehot((lax.shift_right_logical(col, 4) == row) & ((col & 15) == i))
        return carry

    lax.fori_loop(0, NH, build_t, 0)

    lacc_s[...] = jnp.zeros_like(lacc_s)
    lacc[...] = jnp.zeros_like(lacc)

    load_q.wait()
    q_flat = q_in[...].reshape(NS * NH, LAT + 64)
    for g in range(2):
        t_part = tmat[g * 8:(g + 1) * 8].reshape(8 * SP, NS * NH)
        q_t[g * 8:(g + 1) * 8] = nn(t_part, q_flat).astype(BF).reshape(8, SP, LAT + 64)
    pl.semaphore_wait(barrier, PRE - 1 + HEAD - 1)

    def tiles(i):
        return (
            k_hbm.at[:, pl.ds(pl.multiple_of(c * 256 + i * 16, 16), 16), lane(x)],
            k_hbm.at[:, pl.ds(pl.multiple_of(LAT + lax.rem(i, 4) * 16, 16), 16), lane(x)],
        )

    def s1l(other, src):
        return remote(tiles(other)[0], krl.at[pl.ds(src * NSLOT, NSLOT)],
                      a2a_s.at[0, other], a2a_r.at[0, src], other, h)

    def s1r(other, src):
        return remote(tiles(other)[1], krr.at[pl.ds(src * NSLOT, NSLOT)],
                      a2a_s.at[1, other], a2a_r.at[1, src], other, h)

    def on_core0(fn):
        pl.when(c == 0)(lambda: around(fn))

    around(lambda other: s1l(other, p).start())
    on_core0(lambda other: s1r(other, p).start())
    own_l = pltpu.make_async_copy(tiles(p)[0], krl.at[pl.ds(p * NSLOT, NSLOT)], ld_sem.at[0])
    own_r = pltpu.make_async_copy(tiles(p)[1], krr.at[pl.ds(p * NSLOT, NSLOT)], ld_sem.at[1])
    own_l.start()
    own_r.start()

    names = jnp.broadcast_to(prompt_row[...], (SP, PRE * SP))
    at = iota((SP, PRE * SP), 1)
    rank_row[...] = prompt_row[...] * GROUP

    def build_rank(i, carry):
        ids = iota((SP, PRE * SP), 0) + i * SP
        name = jnp.sum(jnp.where(at == ids, names, 0), axis=1, keepdims=True)
        same = names == name
        before = jnp.sum(jnp.where(same & (at < ids), 1, 0), axis=1, keepdims=True)
        rank_col[pl.ds(pl.multiple_of(i * NS, 8), NS)] = (name * GROUP + before)[:NS]
        rank_row[...] += jnp.sum(jnp.where(same & (ids < at), 1, 0), axis=0, keepdims=True)
        return carry

    lax.fori_loop(0, PRE, build_rank, 0)
    def rank_of(place):
        r0 = 80 * lax.shift_right_logical(place, 4) + (place & 15)
        r1 = 80 * lax.shift_right_logical(place - 128, 5) + (place & 31) + 16
        r2 = 80 * lax.shift_right_logical(place - 384, 5) + (place & 31) + 48
        return jnp.where(place < 128, r0, jnp.where(place < 384, r1, r2))

    def build_sort(i, carry):
        rows = pl.ds(pl.multiple_of(i * 64, 64), 64)
        place = iota((64, 1), 0) + i * 64
        sort[rows] = onehot(rank_of(place) == rank_row[...])
        unsort[rows] = onehot(rank_col[rows] == rank_of(iota((1, PRE * NS), 1)))
        return carry

    lax.fori_loop(0, PRE * NS // 64, build_sort, 0)

    load_v.start()
    load_w.start()
    for n in range(NBUF):
        suf_load(n, n).start()

    def suffix_one(n, carry):
        slot = lax.rem(n, NBUF)
        suf_load(n, slot).wait()
        qn = q_in[n]
        kn = sufbuf[slot]
        t = nn(qn, kn) * SCALE2
        t = jnp.where(iota((NH, SUF), 1) < lens[n], t, MASKED)
        m = jnp.max(t, axis=1, keepdims=True)
        w = jnp.exp2(t - m).astype(BF)
        total = jnp.sum(w.astype(F32), axis=1, keepdims=True)
        o = nt(w, kn[:LAT]) / total
        lat_s[pl.ds(pl.multiple_of(n * NH, NH), NH)] = o.astype(BF)
        lse = m + jnp.log2(total)
        lacc_s[...] = jnp.where(iota((NH, 128), 1) == n, lse, lacc_s[...])

        @pl.when(n + NBUF < NS)
        def _():
            suf_load(n + NBUF, slot).start()

        return carry


    around(lambda other: s1l(other, other).wait_recv())
    on_core0(lambda other: s1r(other, other).wait_recv())
    own_l.wait()
    own_r.wait()

    def pick(prompt, carry):
        for b in range(8):
            slot = slots[b, prompt]
            skl[b // 4, prompt * 4 + b % 4] = krl[slot]
        for hf in range(2):
            skr[hf, prompt] = krr[slots[hf * 4 + p // 4, prompt]]
        return carry

    lax.fori_loop(0, NPROMPT, pick, 0)

    def first_of(other):
        return 5 * (other // 8) + lax.rem(other // 2, 4)

    def s2l(ab, other, src):
        rows = pl.ds(pl.multiple_of(c * 256 + src * 16, 16), 16)
        return remote(skl.at[lax.rem(other, 2), pl.ds((first_of(other) + ab) * 4, 4)],
                      kw.at[pl.ds(ab * 4, 4), rows, lane(x)],
                      a2a_s.at[3 + ab, other], a2a_r.at[3 + ab, src], other, h)

    def s2r(other, src):
        rows = pl.ds(pl.multiple_of(LAT + lax.rem(src, 4) * 16, 16), 16)
        return remote(skr.at[lax.rem(other, 2), pl.ds(first_of(other), 2)],
                      kw.reshape(2, 4, LAT + 64, 512).at[:, src // 4, rows, lane(x)],
                      a2a_s.at[5, other], a2a_r.at[5, src], other, h)

    own = first_of(p)
    for ab in range(2):
        around(lambda other: s2l(ab, other, p).start())
        if ab == 0:
            on_core0(lambda other: s2r(other, p).start())
    kw[:, pl.ds(pl.multiple_of(c * 256 + p * 16, 16), 16), lane(x)] = skl[half, pl.ds(own * 4, 8)]

    @pl.when(c == 0)
    def _():
        rows = pl.ds(pl.multiple_of(LAT + lax.rem(p, 4) * 16, 16), 16)
        kw[p // 4, rows, lane(x)] = skr[half, own]
        kw[p // 4 + 4, rows, lane(x)] = skr[half, own + 1]

    def s1q(other, src):
        return remote(q_t.at[other], qr.at[src], a2a_s.at[2, other], a2a_r.at[2, src], other, h)

    around(lambda other: s1q(other, p).start())
    qr[p] = q_t[p]

    lax.fori_loop(0, 6, suffix_one, 0)

    def views(cc, src_x):
        rows = pl.ds(pl.multiple_of(cc * 256, 256), 256)
        return kw.at[0:4, rows, lane(src_x)], kw.at[4:8, rows, lane(src_x)], kw.at[:, LAT:, lane(src_x)]

    def back(d):
        return lax.rem(x + 4 - d, 4)

    def x_copy(k, d, src_x):
        step = d if d != 2 or k == 2 else (1, 3)[k]
        view = views(c, src_x)[k]
        return remote(view, view, x_s.at[k, d - 1], x_r.at[k, d - 1], p, lax.rem(x + step, 4) * 2 + c)

    def core_copy(k, d, src_x, cc):
        view = views(cc, src_x)[k]
        return remote(view, view, c_s.at[k, d], c_r.at[k, d], p, x * 2 + (1 - c))

    def send_x(k):
        for d in (1, 3) if k < 2 else (1, 3, 2):
            x_copy(k, d, x).start()
        core_copy(k, 0, x, c).start()

    def pass_on(k, d):
        x_copy(k, d, back(d)).wait_recv()
        if (k, d) in ((0, 1), (1, 3)):
            x_copy(k, 2, back(d)).start()
        core_copy(k, d, back(d), c).start()

    def wait_core(k):
        for d in (0, 1, 3, 2):
            core_copy(k, d, back(d), 1 - c).wait_recv()

    def core0(fn):
        pl.when(c == 0)(fn)

    around(lambda other: s2l(0, other, other).wait_recv())
    send_x(0)
    around(lambda other: s2l(1, other, other).wait_recv())
    send_x(1)
    on_core0(lambda other: s2r(other, other).wait_recv())
    core0(lambda: send_x(2))
    lax.fori_loop(6, 12, suffix_one, 0)
    pass_on(0, 1)
    pass_on(0, 3)
    lax.fori_loop(12, 14, suffix_one, 0)

    around(lambda other: s1q(other, other).wait_recv())
    q_all = qr[...].reshape(PRE * SP, LAT + 64)

    def s2q(g, other, src):
        r0, nr, base = GROUPS[g]
        return remote(sq.at[pl.ds(pl.multiple_of(base + (other // 2) * nr, 16), nr)], qw.at[src, pl.ds(r0, nr)],
                      a2a_s.at[6 + g, other], a2a_r.at[6 + g, src], other, h)

    for g, (r0, nr, base) in enumerate(GROUPS):
        sq[base:base + 8 * nr] = nn(sort[base:base + 8 * nr], q_all).astype(BF)
        around(lambda other: s2q(g, other, p).start())
        qw[p, r0:r0 + nr] = sq[pl.ds(pl.multiple_of(base + win * nr, 16), nr)]

    pass_on(1, 3)
    pass_on(1, 1)
    lax.fori_loop(14, 24, suffix_one, 0)
    pass_on(0, 2)
    lax.fori_loop(24, 32, suffix_one, 0)
    pass_on(1, 2)

    @core0
    def _():
        for d in (1, 3, 2):
            pass_on(2, d)

    lax.fori_loop(32, NS, suffix_one, 0)

    load_v.wait()
    for g in range(2):
        t_part = tmat[g * 8:(g + 1) * 8].reshape(8 * SP, NS * NH)
        lt_s[g * 8:(g + 1) * 8] = nn(t_part, lat_s[...]).astype(BF).reshape(8, SP, LAT)

    def project_s(i, carry):
        o_s[i] = nn(lt_s[i], vm[i]).astype(BF)
        return carry

    lax.fori_loop(0, NH, project_s, 0)
    l_s[...] = lacc_s[...][:, None, :]

    def s4o(other, src):
        return remote(o_s.at[other], osr.at[src], a2a_s.at[9, other], a2a_r.at[9, src], other, h)

    def s4l(other, src):
        return remote(l_s.at[other], lsr.at[src], a2a_s.at[10, other], a2a_r.at[10, src], other, h)

    def start4(other):
        s4o(other, p).start()
        s4l(other, p).start()

    around(start4)
    osr[p] = o_s[p]
    lsr[p] = l_s[p]

    def spread(src, carry):
        rows = pl.ds(pl.multiple_of(src * SP, 16), SP)
        suf_rhs[rows, :VD] = osr[src]
        row = jnp.broadcast_to(lsr[src], (SP, 128))
        at = iota((SP, 128), 1)
        lse = jnp.sum(jnp.where(iota((SP, 128), 0) == at, row, 0.0), axis=1, keepdims=True)
        high = lse.astype(BF).astype(F32)
        middle = (lse - high).astype(BF).astype(F32)
        low = lse - high - middle
        terms = jnp.where(at == 0, high, jnp.where(at == 1, middle, jnp.where(at == 2, low, 0.0)))
        suf_rhs[rows, VD:] = terms.astype(BF)
        return carry

    def sort_suffix():
        def wait4(other):
            s4o(other, other).wait_recv()
            s4l(other, other).wait_recv()

        around(wait4)
        lax.fori_loop(0, PRE, spread, 0)
        suf[...] = nn(sort[...], suf_rhs[...])

    def chunk(g, t, carry):
        rows = pl.ds(pl.multiple_of(t * 16, 16), 16)
        ab = (t + wj) // 4
        qc = qw[:, rows].reshape(256, LAT + 64)
        scores = [nn(qc, kw[ab * 4 + b]) * SCALE2 for b in range(4)]
        m = functools.reduce(jnp.maximum, [jnp.max(t, axis=1, keepdims=True) for t in scores])
        total = jnp.zeros((256, 1), F32)
        acc = jnp.zeros((256, LAT), F32)
        for b in range(4):
            w = jnp.exp2(scores[b] - m).astype(BF)
            total = total + jnp.sum(w.astype(F32), axis=1, keepdims=True)
            acc = acc + nt(w, kw[ab * 4 + b, :LAT])
        ol[:, rows] = (acc / total).astype(BF).reshape(NH, 16, LAT)
        lse = (m + jnp.log2(total)).reshape(NH, 16, 1)
        here = iota((NH, 16, 128), 2) == iota((NH, 16, 128), 1) + (t * 16 - GROUPS[g][0])
        lacc[g] += jnp.sum(jnp.where(here, lse, 0.0), axis=1)
        return carry

    def s5o(g, other, src):
        r0, nr, base = GROUPS[g]
        rows = pl.ds(pl.multiple_of(base + (src // 2) * nr, 16), nr)
        return remote(op.at[other, pl.ds(r0, nr)], orr.at[rows, lane(lax.rem(src, 2))],
                      a2a_s.at[11 + g, other], a2a_r.at[11 + g, src], other, h)

    def s5l(g, other, src):
        return remote(lps.at[g, other], lr.at[g, lax.rem(src, 2), src // 2],
                      a2a_s.at[14 + g, other], a2a_r.at[14 + g, src], other, h)

    def attend(g):
        r0, nr, base = GROUPS[g]
        around(lambda other: s2q(g, other, other).wait_recv())
        lax.fori_loop(r0 // 16, (r0 + nr) // 16, functools.partial(chunk, g), 0)
        lps[g] = lacc[g][:, None, :]

        def start5(other):
            op[other, r0:r0 + nr] = nn(ol[other, r0:r0 + nr], vm[other]).astype(BF)
            s5o(g, other, p).start()
            s5l(g, other, p).start()

        around(start5)
        orr[pl.ds(pl.multiple_of(base + win * nr, 16), nr), lane(half)] = nn(ol[p, r0:r0 + nr], vm[p]).astype(BF)
        lr[g, half, win] = lps[g, p]

    def merge(g):
        r0, nr, base = GROUPS[g]

        def wait5(other):
            s5o(g, other, other).wait_recv()
            s5l(g, other, other).wait_recv()

        around(wait5)
        rows = slice(base, base + 8 * nr)
        eye = iota((8, nr, 128), 2) == iota((8, nr, 128), 1)

        def column(hf):
            spread_l = jnp.where(eye, jnp.broadcast_to(lr[g, hf], (8, nr, 128)), 0.0)
            return jnp.sum(spread_l, axis=2, keepdims=True).reshape(8 * nr, 1)

        la, lb = column(0), column(1)
        ls = jnp.sum(suf[rows, VD:], axis=1, keepdims=True)
        top = jnp.maximum(jnp.maximum(la, lb), ls)
        ea, eb, es = jnp.exp2(la - top), jnp.exp2(lb - top), jnp.exp2(ls - top)
        inv = 1.0 / (ea + eb + es)
        merged = (
            (ea * inv) * orr[rows, :VD].astype(F32)
            + (eb * inv) * orr[rows, VD:].astype(F32)
            + (es * inv) * suf[rows, :VD]
        )
        hbuf[rows, lane(p)] = merged.astype(BF)

    def g_copy(g, part, piece, dy, dz, ssem, rsem):
        _, nr, base = GROUPS[g]
        view = hbuf.at[pl.ds(base + part * 4 * nr, 4 * nr), lane(piece)]
        return remote(view, view, ssem, rsem, lax.rem(y + dy, 4) * 4 + lax.rem(z + dz, 4), h)

    def piece_of(by, bz):
        return lax.rem(y + 4 - by, 4) * 4 + lax.rem(z + 4 - bz, 4)

    def first(g, part, d, piece):
        dy, dz = (0, d) if part == 0 else (d, 0)
        return g_copy(g, part, piece, dy, dz, g1_s.at[g, part, d - 1], g1_r.at[g, part, d - 1])

    def second(g, part, k, d, piece):
        dy, dz = (d, 0) if part == 0 else (0, d)
        return g_copy(g, part, piece, dy, dz, g2_s.at[g, part, k * 3 + d - 1], g2_r.at[g, part, k * 3 + d - 1])

    def gather1(g):
        for d in (1, 3, 2):
            for part in range(2):
                first(g, part, d, p).start()
        for d in (1, 3, 2):
            for part in range(2):
                second(g, part, 0, d, p).start()

    def gather2(g):
        for k in (1, 3, 2):
            for part in range(2):
                got = piece_of(0, k) if part == 0 else piece_of(k, 0)
                first(g, part, k, got).wait_recv()
                for d in (1, 3, 2):
                    second(g, part, k, d, got).start()

    def gathered(g):
        for k in (0, 1, 3, 2):
            for d in (1, 3, 2):
                for part in range(2):
                    got = piece_of(d, k) if part == 0 else piece_of(k, d)
                    second(g, part, k, d, got).wait_recv()

    def out_rows(g):
        _, nr, base = GROUPS[g]
        rows = slice(base, base + 8 * nr)
        part_o[rows] = nt(hbuf[rows], w_in[...]).astype(BF)

    wait_core(0)
    wait_core(1)
    pl.when(c == 1)(lambda: wait_core(2))
    attend(0)
    sort_suffix()
    attend(1)
    merge(0)
    gather1(0)
    attend(2)
    gather2(0)
    merge(1)
    gather1(1)
    load_w.wait()
    gathered(0)
    out_rows(0)
    merge(2)
    gather1(2)
    gather2(1)
    gather2(2)
    gathered(1)
    out_rows(1)
    gathered(2)
    out_rows(2)

    for g in range(2):
        pb[g * 4:(g + 1) * 4] = nn(unsort[g * 320:(g + 1) * 320], part_o[...]).astype(BF).reshape(4, WIN, 448)

    def s6(other, src):
        return remote(pb.at[other], rs.at[src], e_s.at[other], e_r.at[src], p, other)

    def heads(fn):
        def body(d, carry):
            fn(lax.rem(h + d, HEAD))
            return carry
        lax.fori_loop(1, HEAD, body, 0)

    heads(lambda other: s6(other, h).start())
    rs[h] = pb[h]
    heads(lambda other: s6(other, other).wait_recv())
    total = rs[0].astype(F32)
    for k in range(1, HEAD):
        total = total + rs[k].astype(F32)
    out[...] = total.astype(BF)

    def sent(other):
        for copy in (s1l, s1q, s4o, s4l):
            copy(other, p).wait_send()
        for ab in range(2):
            s2l(ab, other, p).wait_send()
        for g in range(3):
            for copy in (s2q, s5o, s5l):
                copy(g, other, p).wait_send()

    around(sent)
    on_core0(lambda other: s1r(other, p).wait_send())
    on_core0(lambda other: s2r(other, p).wait_send())

    def sent_blocks(k):
        for d in (1, 2, 3):
            x_copy(k, d, x).wait_send()
        for d in range(4):
            core_copy(k, d, back(d), c).wait_send()

    sent_blocks(0)
    sent_blocks(1)
    core0(lambda: sent_blocks(2))
    for g in range(3):
        for part in range(2):
            for d in (1, 2, 3):
                first(g, part, d, p).wait_send()
            for k in range(4):
                for d in (1, 2, 3):
                    second(g, part, k, d, p).wait_send()
    heads(lambda other: s6(other, h).wait_send())


def per_device(
    query_latent, prefix_cache, block_slot, sample_prompt, suffix_cache, suffix_length, value_map, out_weight
):
    prompt_row = jnp.pad(
        sample_prompt.reshape(PRE, NS), ((0, 0), (0, SP - NS)), constant_values=-4
    ).reshape(1, PRE * SP)
    vmem = pl.BlockSpec(memory_space=pltpu.VMEM)
    smem = pl.BlockSpec(memory_space=pltpu.SMEM)
    hbm = pl.BlockSpec(memory_space=pl.ANY)
    V = pltpu.VMEM
    dma = pltpu.SemaphoreType.DMA
    width = LAT + 64
    scratch = [
        V((NS, NH, width), BF), V((NH, LAT, VD), BF), V((448, NH * VD), BF),
        V((NBUF, width, SUF), BF),
        V((NH, SP, NS * NH), BF), V((NH, SP, width), BF), V((PRE, SP, width), BF),
        V((PRE * NSLOT, 16, 128), BF), V((PRE * NSLOT, 16, 128), BF),
        V((2, NPROMPT * 4, 16, 128), BF), V((2, NPROMPT, 16, 128), BF),
        V((PRE * NS, width), BF), V((NH, WIN, width), BF),
        V((8, width, 512), BF), V((1, PRE * SP), jnp.int32), V((PRE * NS, 1), jnp.int32),
        V((PRE * NS, PRE * SP), BF), V((PRE * NS, PRE * NS), BF),
        V((NS * NH, LAT), BF), V((NH, SP, LAT), BF), V((NH, SP, VD), BF), V((NH, 1, 128), F32),
        V((PRE, SP, VD), BF), V((PRE, 1, 128), F32), V((NH, 128), F32),
        V((NH, WIN, LAT), BF), V((NH, WIN, VD), BF), V((3, NH, 1, 128), F32),
        V((PRE * NS, 2 * VD), BF), V((3, 2, 8, 1, 128), F32), V((3, NH, 128), F32),
        V((PRE * SP, 2 * VD), BF), V((PRE * NS, 2 * VD), F32), V((PRE * NS, NH * VD), BF),
        V((PRE * NS, 448), BF), V((HEAD, WIN, 448), BF), V((HEAD, WIN, 448), BF),
        dma((5,)), dma((NBUF,)), dma((17, PRE)), dma((17, PRE)),
        dma((3, 3)), dma((3, 3)), dma((3, 4)), dma((3, 4)),
        dma((3, 2, 3)), dma((3, 2, 3)), dma((3, 2, 12)), dma((3, 2, 12)), dma((HEAD,)), dma((HEAD,)),
    ]
    return pl.pallas_call(
        kernel,
        out_shape=jax.ShapeDtypeStruct((WIN, 448), BF),
        in_specs=[hbm, hbm, hbm, hbm, hbm, vmem, smem, smem],
        out_specs=vmem,
        scratch_shapes=scratch,
        compiler_params=pltpu.CompilerParams(
            collective_id=0, has_side_effects=True, vmem_limit_bytes=58 * 1024 * 1024
        ),
        cost_estimate=pl.CostEstimate(flops=10_000_000_000, bytes_accessed=30_000_000, transcendentals=3_000_000),
    )(
        query_latent, prefix_cache.transpose(0, 2, 1), suffix_cache.transpose(0, 2, 1), value_map, out_weight.T,
        prompt_row, block_slot.T, suffix_length,
    )


def solution(mesh):
    return jax.shard_map(
        per_device,
        mesh=mesh,
        in_specs=(
            P("pre", "head", None),
            P("pre", None, None),
            P(),
            P(),
            P("pre", None, None),
            P("pre"),
            P("head", None, None),
            P("head", "pre"),
        ),
        out_specs=P("head", "pre"),
        check_vma=False,
    )
```

```python
import functools
import math

import jax
import jax.numpy as jnp
from jax import lax
from jax.experimental import pallas as pl
from jax.experimental.pallas import tpu as pltpu
from jax.sharding import PartitionSpec as P

GROUP = 64
PRE = 16
HEAD = 8
NS = 40
SP = 48
NH = 16
LAT = 512
VD = 128
SUF = 384
WIN = 80
NSLOT = 5
NPROMPT = 10
NBUF = 4
MASKED = -1e30
GROUPS = ((0, 16, 0), (16, 32, 128), (48, 32, 384))
SCALE2 = math.log2(math.e) / math.sqrt(192.0)

BF = jnp.bfloat16
F32 = jnp.float32
MESH = pl.DeviceIdType.MESH


def nt(a, b):
    return lax.dot_general(a, b, (((1,), (1,)), ((), ())), preferred_element_type=F32)


def nn(a, b):
    return lax.dot_general(a, b, (((1,), (0,)), ((), ())), preferred_element_type=F32)


def onehot(mask):
    return jnp.where(mask, 1.0, 0.0).astype(BF)


def iota(shape, dim):
    return lax.broadcasted_iota(jnp.int32, shape, dim)


def kernel(
    q_hbm, k_hbm, suf_hbm, vm_hbm, w_hbm, prompt_row, slots, lens,
    out,
    q_in, vm, w_in, sufbuf,
    tmat, q_t, qr, krl, krr,
    skl, skr, sq, qw, kw, rank_row, rank_col, sort, unsort,
    lat_s, lt_s, o_s, l_s, osr, lsr, lacc_s,
    ol, op, lps, orr, lr, lacc,
    suf_rhs, suf, hbuf, part_o, pb, cb, xb, rs,
    ld_sem, suf_sem, a2a_s, a2a_r, x_s, x_r, c_s, c_r, g1_s, g1_r, g2_s, g2_r, e_s, e_r,
):
    p = lax.axis_index("pre")
    h = lax.axis_index("head")
    x, c = h // 2, lax.rem(h, 2)
    y, z = p // 4, lax.rem(p, 4)
    win, half = p // 2, lax.rem(p, 2)
    wj = lax.rem(win, 4)

    def remote(src, dst, ssem, rsem, pre, head):
        return pltpu.make_async_remote_copy(
            src_ref=src, dst_ref=dst, send_sem=ssem, recv_sem=rsem,
            device_id={"pre": pre, "head": head}, device_id_type=MESH,
        )

    def around(fn):
        def body(d, carry):
            fn(lax.rem(p + d, PRE))
            return carry
        lax.fori_loop(1, PRE, body, 0)

    def lane(i):
        return pl.ds(pl.multiple_of(i * 128, 128), 128)

    load_q = pltpu.make_async_copy(q_hbm, q_in, ld_sem.at[4])
    load_v = pltpu.make_async_copy(vm_hbm, vm, ld_sem.at[2])
    load_w = pltpu.make_async_copy(w_hbm, w_in, ld_sem.at[3])
    load_q.start()

    def suf_load(n, slot):
        return pltpu.make_async_copy(suf_hbm.at[n], sufbuf.at[slot], suf_sem.at[slot])

    barrier = pltpu.get_barrier_semaphore()

    def greet_pre(other):
        pl.semaphore_signal(barrier, inc=1, device_id={"pre": other, "head": h}, device_id_type=MESH)

    around(greet_pre)

    def greet_head(d, carry):
        pl.semaphore_signal(
            barrier, inc=1, device_id={"pre": p, "head": lax.rem(h + d, HEAD)}, device_id_type=MESH
        )
        return carry

    lax.fori_loop(1, HEAD, greet_head, 0)

    lacc_s[...] = jnp.zeros_like(lacc_s)
    lacc[...] = jnp.zeros_like(lacc)

    pl.semaphore_wait(barrier, PRE - 1 + HEAD - 1)

    def tiles(i):
        return (
            k_hbm.at[:, pl.ds(pl.multiple_of(c * 256 + i * 16, 16), 16), lane(x)],
            k_hbm.at[:, pl.ds(pl.multiple_of(LAT + lax.rem(i, 4) * 16, 16), 16), lane(x)],
        )

    def s1l(other, src):
        return remote(tiles(other)[0], krl.at[pl.ds(src * NSLOT, NSLOT)],
                      a2a_s.at[0, other], a2a_r.at[0, src], other, h)

    def s1r(other, src):
        return remote(tiles(other)[1], krr.at[pl.ds(src * NSLOT, NSLOT)],
                      a2a_s.at[1, other], a2a_r.at[1, src], other, h)

    def on_core0(fn):
        pl.when(c == 0)(lambda: around(fn))

    around(lambda other: s1l(other, p).start())
    on_core0(lambda other: s1r(other, p).start())
    own_l = pltpu.make_async_copy(tiles(p)[0], krl.at[pl.ds(p * NSLOT, NSLOT)], ld_sem.at[0])
    own_r = pltpu.make_async_copy(tiles(p)[1], krr.at[pl.ds(p * NSLOT, NSLOT)], ld_sem.at[1])
    own_l.start()
    own_r.start()

    def build_t(i, carry):
        row = iota((SP, NS * NH), 0)
        col = iota((SP, NS * NH), 1)
        tmat[i] = onehot((lax.shift_right_logical(col, 4) == row) & ((col & 15) == i))
        return carry

    lax.fori_loop(0, NH, build_t, 0)

    load_q.wait()
    q_flat = q_in[...].reshape(NS * NH, LAT + 64)
    for g in range(2):
        t_part = tmat[g * 8:(g + 1) * 8].reshape(8 * SP, NS * NH)
        q_t[g * 8:(g + 1) * 8] = nn(t_part, q_flat).astype(BF).reshape(8, SP, LAT + 64)
    names = jnp.broadcast_to(prompt_row[...], (SP, PRE * SP))
    at = iota((SP, PRE * SP), 1)
    rank_row[...] = prompt_row[...] * GROUP

    def build_rank(i, carry):
        ids = iota((SP, PRE * SP), 0) + i * SP
        name = jnp.sum(jnp.where(at == ids, names, 0), axis=1, keepdims=True)
        same = names == name
        before = jnp.sum(jnp.where(same & (at < ids), 1, 0), axis=1, keepdims=True)
        rank_col[pl.ds(pl.multiple_of(i * NS, 8), NS)] = (name * GROUP + before)[:NS]
        rank_row[...] += jnp.sum(jnp.where(same & (ids < at), 1, 0), axis=0, keepdims=True)
        return carry

    lax.fori_loop(0, PRE, build_rank, 0)
    def rank_of(place):
        r0 = 80 * lax.shift_right_logical(place, 4) + (place & 15)
        r1 = 80 * lax.shift_right_logical(place - 128, 5) + (place & 31) + 16
        r2 = 80 * lax.shift_right_logical(place - 384, 5) + (place & 31) + 48
        return jnp.where(place < 128, r0, jnp.where(place < 384, r1, r2))

    def build_sort(i, carry):
        rows = pl.ds(pl.multiple_of(i * 64, 64), 64)
        place = iota((64, 1), 0) + i * 64
        sort[rows] = onehot(rank_of(place) == rank_row[...])
        unsort[rows] = onehot(rank_col[rows] == rank_of(iota((1, PRE * NS), 1)))
        return carry

    lax.fori_loop(0, PRE * NS // 64, build_sort, 0)

    load_v.start()
    load_w.start()
    for n in range(NBUF):
        suf_load(n, n).start()

    def suffix_pair(pair, carry):
        ns = (2 * pair, 2 * pair + 1)
        slots_of = [lax.rem(n, NBUF) for n in ns]
        for n, slot in zip(ns, slots_of):
            suf_load(n, slot).wait()
        keys = [sufbuf[slot] for slot in slots_of]
        ts = [nn(q_in[n], kn) * SCALE2 for n, kn in zip(ns, keys)]
        ts = [jnp.where(iota((NH, SUF), 1) < lens[n], t, MASKED) for n, t in zip(ns, ts)]
        ms = [jnp.max(t, axis=1, keepdims=True) for t in ts]
        ws = [jnp.exp2(t - m).astype(BF) for t, m in zip(ts, ms)]
        totals = [jnp.sum(w.astype(F32), axis=1, keepdims=True) for w in ws]
        outs = [nt(w, kn[:LAT]) for w, kn in zip(ws, keys)]
        both = jnp.concatenate([o / total for o, total in zip(outs, totals)], axis=0)
        lat_s[pl.ds(pl.multiple_of(pair * 2 * NH, 2 * NH), 2 * NH)] = both.astype(BF)
        at = iota((NH, 128), 1)
        lse = [m + jnp.log2(total) for m, total in zip(ms, totals)]
        lacc_s[...] = jnp.where(at == ns[0], lse[0], jnp.where(at == ns[1], lse[1], lacc_s[...]))

        @pl.when(ns[0] + NBUF < NS)
        def _():
            for n, slot in zip(ns, slots_of):
                suf_load(n + NBUF, slot).start()

        return carry

    def suffix(first, last):
        lax.fori_loop(first // 2, last // 2, suffix_pair, 0)

    around(lambda other: s1l(other, other).wait_recv())
    on_core0(lambda other: s1r(other, other).wait_recv())
    own_l.wait()
    own_r.wait()

    def pick(prompt, carry):
        for b in range(8):
            slot = slots[b, prompt]
            skl[b // 4, prompt * 4 + b % 4] = krl[slot]
        for hf in range(2):
            skr[hf, prompt] = krr[slots[hf * 4 + p // 4, prompt]]
        return carry

    lax.fori_loop(0, NPROMPT, pick, 0)

    def first_of(other):
        return 5 * (other // 8) + lax.rem(other // 2, 4)

    def s2l(ab, other, src):
        rows = pl.ds(pl.multiple_of(c * 256 + src * 16, 16), 16)
        return remote(skl.at[lax.rem(other, 2), pl.ds((first_of(other) + ab) * 4, 4)],
                      kw.at[pl.ds(ab * 4, 4), rows, lane(x)],
                      a2a_s.at[3 + ab, other], a2a_r.at[3 + ab, src], other, h)

    def s2r(other, src):
        rows = pl.ds(pl.multiple_of(LAT + lax.rem(src, 4) * 16, 16), 16)
        return remote(skr.at[lax.rem(other, 2), pl.ds(first_of(other), 2)],
                      kw.reshape(2, 4, LAT + 64, 512).at[:, src // 4, rows, lane(x)],
                      a2a_s.at[5, other], a2a_r.at[5, src], other, h)

    own = first_of(p)
    for ab in range(2):
        around(lambda other: s2l(ab, other, p).start())
        if ab == 0:
            on_core0(lambda other: s2r(other, p).start())
    kw[:, pl.ds(pl.multiple_of(c * 256 + p * 16, 16), 16), lane(x)] = skl[half, pl.ds(own * 4, 8)]

    @pl.when(c == 0)
    def _():
        rows = pl.ds(pl.multiple_of(LAT + lax.rem(p, 4) * 16, 16), 16)
        kw[p // 4, rows, lane(x)] = skr[half, own]
        kw[p // 4 + 4, rows, lane(x)] = skr[half, own + 1]

    def s1q(other, src):
        return remote(q_t.at[other], qr.at[src], a2a_s.at[2, other], a2a_r.at[2, src], other, h)

    around(lambda other: s1q(other, p).start())
    qr[p] = q_t[p]

    suffix(0, 6)

    def views(cc, src_x):
        rows = pl.ds(pl.multiple_of(cc * 256, 256), 256)
        return kw.at[0:4, rows, lane(src_x)], kw.at[4:8, rows, lane(src_x)], kw.at[:, LAT:, lane(src_x)]

    def back(d):
        return lax.rem(x + 4 - d, 4)

    def x_copy(k, d, src_x):
        step = d if d != 2 or k == 2 else (1, 3)[k]
        view = views(c, src_x)[k]
        return remote(view, view, x_s.at[k, d - 1], x_r.at[k, d - 1], p, lax.rem(x + step, 4) * 2 + c)

    def core_copy(k, d, src_x, cc):
        view = views(cc, src_x)[k]
        return remote(view, view, c_s.at[k, d], c_r.at[k, d], p, x * 2 + (1 - c))

    def send_x(k):
        for d in (1, 3) if k < 2 else (1, 3, 2):
            x_copy(k, d, x).start()
        core_copy(k, 0, x, c).start()

    def pass_on(k, d):
        x_copy(k, d, back(d)).wait_recv()
        if (k, d) in ((0, 1), (1, 3)):
            x_copy(k, 2, back(d)).start()
        core_copy(k, d, back(d), c).start()

    def wait_core(k):
        for d in (0, 1, 3, 2):
            core_copy(k, d, back(d), 1 - c).wait_recv()

    def core0(fn):
        pl.when(c == 0)(fn)

    around(lambda other: s2l(0, other, other).wait_recv())
    send_x(0)
    on_core0(lambda other: s2r(other, other).wait_recv())
    core0(lambda: send_x(2))
    around(lambda other: s2l(1, other, other).wait_recv())
    send_x(1)
    suffix(6, 12)
    pass_on(0, 1)
    pass_on(0, 3)
    suffix(12, 18)

    around(lambda other: s1q(other, other).wait_recv())
    q_all = qr[...].reshape(PRE * SP, LAT + 64)

    def s2q(g, other, src):
        r0, nr, base = GROUPS[g]
        return remote(sq.at[pl.ds(pl.multiple_of(base + (other // 2) * nr, 16), nr)], qw.at[src, pl.ds(r0, nr)],
                      a2a_s.at[6 + g, other], a2a_r.at[6 + g, src], other, h)

    for g, (r0, nr, base) in enumerate(GROUPS):
        sq[base:base + 8 * nr] = nn(sort[base:base + 8 * nr], q_all).astype(BF)
        if g == 0:
            around(lambda other: s2q(g, other, p).start())
        qw[p, r0:r0 + nr] = sq[pl.ds(pl.multiple_of(base + win * nr, 16), nr)]

    @core0
    def _():
        for d in (1, 3, 2):
            pass_on(2, d)

    def next_group(g):
        around(lambda other: s2q(g - 1, other, p).wait_send())
        around(lambda other: s2q(g, other, p).start())

    pass_on(1, 3)
    suffix(18, 22)
    next_group(1)
    suffix(22, 26)
    pass_on(0, 2)
    pass_on(1, 1)
    suffix(26, 34)
    next_group(2)
    suffix(34, NS)

    def s4o(other, src):
        return remote(o_s.at[other], osr.at[src], a2a_s.at[9, other], a2a_r.at[9, src], other, h)

    def s4l(other, src):
        return remote(l_s.at[other], lsr.at[src], a2a_s.at[10, other], a2a_r.at[10, src], other, h)

    def start4(other):
        s4o(other, p).start()
        s4l(other, p).start()

    def spread(src, carry):
        rows = pl.ds(pl.multiple_of(src * SP, 16), SP)
        suf_rhs[rows, :VD] = osr[src]
        row = jnp.broadcast_to(lsr[src], (SP, 128))
        at = iota((SP, 128), 1)
        lse = jnp.sum(jnp.where(iota((SP, 128), 0) == at, row, 0.0), axis=1, keepdims=True)
        high = lse.astype(BF).astype(F32)
        middle = (lse - high).astype(BF).astype(F32)
        low = lse - high - middle
        terms = jnp.where(at == 0, high, jnp.where(at == 1, middle, jnp.where(at == 2, low, 0.0)))
        suf_rhs[rows, VD:] = terms.astype(BF)
        return carry

    def sort_suffix():
        def wait4(other):
            s4o(other, other).wait_recv()
            s4l(other, other).wait_recv()

        around(wait4)
        lax.fori_loop(0, PRE, spread, 0)
        suf[...] = nn(sort[...], suf_rhs[...])

    def chunk(g, t, carry):
        rows = pl.ds(pl.multiple_of(t * 16, 16), 16)
        ab = (t + wj) // 4
        qc = qw[:, rows].reshape(256, LAT + 64)
        scores = [nn(qc, kw[ab * 4 + b]) * SCALE2 for b in range(4)]
        m = functools.reduce(jnp.maximum, [jnp.max(t, axis=1, keepdims=True) for t in scores])
        total = jnp.zeros((256, 1), F32)
        acc = jnp.zeros((256, LAT), F32)
        for b in range(4):
            w = jnp.exp2(scores[b] - m).astype(BF)
            total = total + jnp.sum(w.astype(F32), axis=1, keepdims=True)
            acc = acc + nt(w, kw[ab * 4 + b, :LAT])
        ol[:, rows] = (acc / total).astype(BF).reshape(NH, 16, LAT)
        lse = (m + jnp.log2(total)).reshape(NH, 16, 1)
        here = iota((NH, 16, 128), 2) == iota((NH, 16, 128), 1) + (t * 16 - GROUPS[g][0])
        lacc[g] += jnp.sum(jnp.where(here, lse, 0.0), axis=1)
        return carry

    def s5o(g, other, src):
        r0, nr, base = GROUPS[g]
        rows = pl.ds(pl.multiple_of(base + (src // 2) * nr, 16), nr)
        return remote(op.at[other, pl.ds(r0, nr)], orr.at[rows, lane(lax.rem(src, 2))],
                      a2a_s.at[11 + g, other], a2a_r.at[11 + g, src], other, h)

    def s5l(g, other, src):
        return remote(lps.at[g, other], lr.at[g, lax.rem(src, 2), src // 2],
                      a2a_s.at[14 + g, other], a2a_r.at[14 + g, src], other, h)

    def attend(g):
        r0, nr, base = GROUPS[g]
        around(lambda other: s2q(g, other, other).wait_recv())
        lax.fori_loop(r0 // 16, (r0 + nr) // 16, functools.partial(chunk, g), 0)
        lps[g] = lacc[g][:, None, :]

        for i in range(NH):
            op[i, r0:r0 + nr] = nn(ol[i, r0:r0 + nr], vm[i]).astype(BF)

        def start5(other):
            s5o(g, other, p).start()
            s5l(g, other, p).start()

        around(start5)
        orr[pl.ds(pl.multiple_of(base + win * nr, 16), nr), lane(half)] = op[p, r0:r0 + nr]
        lr[g, half, win] = lps[g, p]

    def merge(g):
        r0, nr, base = GROUPS[g]

        def wait5(other):
            s5o(g, other, other).wait_recv()
            s5l(g, other, other).wait_recv()

        around(wait5)
        rows = slice(base, base + 8 * nr)
        eye = iota((8, nr, 128), 2) == iota((8, nr, 128), 1)

        def column(hf):
            spread_l = jnp.where(eye, jnp.broadcast_to(lr[g, hf], (8, nr, 128)), 0.0)
            return jnp.sum(spread_l, axis=2, keepdims=True).reshape(8 * nr, 1)

        la, lb = column(0), column(1)
        ls = jnp.sum(suf[rows, VD:], axis=1, keepdims=True)
        top = jnp.maximum(jnp.maximum(la, lb), ls)
        ea, eb, es = jnp.exp2(la - top), jnp.exp2(lb - top), jnp.exp2(ls - top)
        inv = 1.0 / (ea + eb + es)
        merged = (
            (ea * inv) * orr[rows, :VD].astype(F32)
            + (eb * inv) * orr[rows, VD:].astype(F32)
            + (es * inv) * suf[rows, :VD]
        )
        hbuf[y, z, rows] = merged.astype(BF)

    def half_rows(g, part):
        _, nr, base = GROUPS[g]
        return pl.ds(base + part * 4 * nr, 4 * nr)

    def first(g, part, d, src_y, src_z):
        dy, dz = (0, d) if part == 0 else (d, 0)
        view = hbuf.at[src_y, src_z, half_rows(g, part)]
        return remote(view, view, g1_s.at[g, part, d - 1], g1_r.at[g, part, d - 1],
                      lax.rem(y + dy, 4) * 4 + lax.rem(z + dz, 4), h)

    def second(g, part, d, src):
        rows = half_rows(g, part)
        dy, dz = (d, 0) if part == 0 else (0, d)
        view = hbuf.at[src, :, rows] if part == 0 else hbuf.at[:, src, rows]
        return remote(view, view, g2_s.at[g, part, d - 1], g2_r.at[g, part, d - 1],
                      lax.rem(y + dy, 4) * 4 + lax.rem(z + dz, 4), h)

    def gather1(g):
        for d in (2, 1, 3):
            for part in range(2):
                first(g, part, d, y, z).start()

    def gather2(g):
        for part in range(2):
            for d in (1, 3, 2):
                at_z = lax.rem(z + 4 - d, 4) if part == 0 else z
                at_y = lax.rem(y + 4 - d, 4) if part == 1 else y
                first(g, part, d, at_y, at_z).wait_recv()
            for d in (2, 1, 3):
                second(g, part, d, (y, z)[part]).start()

    def gathered(g):
        for d in (1, 3, 2):
            for part in range(2):
                second(g, part, d, lax.rem((y, z)[part] + 4 - d, 4)).wait_recv()

    def out_rows(g):
        _, nr, base = GROUPS[g]
        rows = slice(base, base + 8 * nr)
        merged = jnp.concatenate([hbuf[k // 4, k % 4, rows] for k in range(PRE)], axis=1)
        part_o[rows] = nt(merged, w_in[...]).astype(BF)

    pass_on(1, 2)
    wait_core(0)
    pl.when(c == 1)(lambda: wait_core(2))
    load_v.wait()
    attend(0)
    for g in range(2):
        t_part = tmat[g * 8:(g + 1) * 8].reshape(8 * SP, NS * NH)
        lt_s[g * 8:(g + 1) * 8] = nn(t_part, lat_s[...]).astype(BF).reshape(8, SP, LAT)

    for i in range(NH):
        o_s[i] = nn(lt_s[i], vm[i]).astype(BF)
    l_s[...] = lacc_s[...][:, None, :]

    around(start4)
    osr[p] = o_s[p]
    lsr[p] = l_s[p]

    wait_core(1)
    attend(1)
    sort_suffix()
    merge(0)
    gather1(0)
    attend(2)
    gather2(0)
    merge(1)
    gather1(1)
    merge(2)
    gather1(2)
    gather2(1)
    load_w.wait()
    gathered(0)
    out_rows(0)
    gather2(2)
    gathered(1)
    out_rows(1)
    gathered(2)
    out_rows(2)

    for g in range(2):
        rows = nn(unsort[g * 320:(g + 1) * 320], part_o[...]).astype(BF)
        for k in range(4):
            pb[k % 2, g * 2 + k // 2] = rows[k * WIN:(k + 1) * WIN]
    swap = remote(pb.at[1 - c], cb, e_s.at[0], e_r.at[0], p, x * 2 + (1 - c))
    swap.start()
    swap.wait_recv()

    def s6(d, src_x):
        to = lax.rem(x + d, 4)
        return remote(xb.at[to], rs.at[src_x], e_s.at[d], e_r.at[d], p, to * 2 + c)

    for d in (2, 1, 3):
        to = lax.rem(x + d, 4)
        xb[to] = (pb[c, to].astype(F32) + cb[to].astype(F32)).astype(BF)
        s6(d, x).start()
    def sent(other):
        for copy in (s1l, s1q, s4o, s4l):
            copy(other, p).wait_send()
        for ab in range(2):
            s2l(ab, other, p).wait_send()
        for g in range(3):
            for copy in (s5o, s5l):
                copy(g, other, p).wait_send()
        s2q(2, other, p).wait_send()

    around(sent)
    on_core0(lambda other: s1r(other, p).wait_send())
    on_core0(lambda other: s2r(other, p).wait_send())

    def sent_blocks(k):
        for d in (1, 2, 3):
            x_copy(k, d, x).wait_send()
        for d in range(4):
            core_copy(k, d, back(d), c).wait_send()

    sent_blocks(0)
    sent_blocks(1)
    core0(lambda: sent_blocks(2))
    for g in range(3):
        for part in range(2):
            for d in (1, 2, 3):
                first(g, part, d, y, z).wait_send()
                second(g, part, d, (y, z)[part]).wait_send()

    total = pb[c, x].astype(F32) + cb[x].astype(F32)
    for d in (1, 3, 2):
        s6(d, back(d)).wait_recv()
        total = total + rs[back(d)].astype(F32)
    out[...] = total.astype(BF)

    swap.wait_send()
    for d in (1, 2, 3):
        s6(d, x).wait_send()


def per_device(
    query_latent, prefix_cache, block_slot, sample_prompt, suffix_cache, suffix_length, value_map, out_weight
):
    prompt_row = jnp.pad(
        sample_prompt.reshape(PRE, NS), ((0, 0), (0, SP - NS)), constant_values=-4
    ).reshape(1, PRE * SP)
    vmem = pl.BlockSpec(memory_space=pltpu.VMEM)
    smem = pl.BlockSpec(memory_space=pltpu.SMEM)
    hbm = pl.BlockSpec(memory_space=pl.ANY)
    V = pltpu.VMEM
    dma = pltpu.SemaphoreType.DMA
    width = LAT + 64
    scratch = [
        V((NS, NH, width), BF), V((NH, LAT, VD), BF), V((448, NH * VD), BF),
        V((NBUF, width, SUF), BF),
        V((NH, SP, NS * NH), BF), V((NH, SP, width), BF), V((PRE, SP, width), BF),
        V((PRE * NSLOT, 16, 128), BF), V((PRE * NSLOT, 16, 128), BF),
        V((2, NPROMPT * 4, 16, 128), BF), V((2, NPROMPT, 16, 128), BF),
        V((PRE * NS, width), BF), V((NH, WIN, width), BF),
        V((8, width, 512), BF), V((1, PRE * SP), jnp.int32), V((PRE * NS, 1), jnp.int32),
        V((PRE * NS, PRE * SP), BF), V((PRE * NS, PRE * NS), BF),
        V((NS * NH, LAT), BF), V((NH, SP, LAT), BF), V((NH, SP, VD), BF), V((NH, 1, 128), F32),
        V((PRE, SP, VD), BF), V((PRE, 1, 128), F32), V((NH, 128), F32),
        V((NH, WIN, LAT), BF), V((NH, WIN, VD), BF), V((3, NH, 1, 128), F32),
        V((PRE * NS, 2 * VD), BF), V((3, 2, 8, 1, 128), F32), V((3, NH, 128), F32),
        V((PRE * SP, 2 * VD), BF), V((PRE * NS, 2 * VD), F32), V((4, 4, PRE * NS, VD), BF),
        V((PRE * NS, 448), BF), V((2, 4, WIN, 448), BF), V((4, WIN, 448), BF), V((4, WIN, 448), BF), V((4, WIN, 448), BF),
        dma((5,)), dma((NBUF,)), dma((17, PRE)), dma((17, PRE)),
        dma((3, 3)), dma((3, 3)), dma((3, 4)), dma((3, 4)),
        dma((3, 2, 3)), dma((3, 2, 3)), dma((3, 2, 3)), dma((3, 2, 3)), dma((4,)), dma((4,)),
    ]
    return pl.pallas_call(
        kernel,
        out_shape=jax.ShapeDtypeStruct((WIN, 448), BF),
        in_specs=[hbm, hbm, hbm, hbm, hbm, vmem, smem, smem],
        out_specs=vmem,
        scratch_shapes=scratch,
        compiler_params=pltpu.CompilerParams(
            collective_id=0, has_side_effects=True, vmem_limit_bytes=58 * 1024 * 1024
        ),
        cost_estimate=pl.CostEstimate(flops=10_000_000_000, bytes_accessed=30_000_000, transcendentals=3_000_000),
    )(
        query_latent, prefix_cache.transpose(0, 2, 1), suffix_cache.transpose(0, 2, 1), value_map, out_weight.T,
        prompt_row, block_slot.T, suffix_length,
    )


def solution(mesh):
    return jax.shard_map(
        per_device,
        mesh=mesh,
        in_specs=(
            P("pre", "head", None),
            P("pre", None, None),
            P(),
            P(),
            P("pre", None, None),
            P("pre"),
            P("head", None, None),
            P("head", "pre"),
        ),
        out_specs=P("head", "pre"),
        check_vma=False,
    )
```

```python
import functools
import math

import jax
import jax.numpy as jnp
from jax import lax
from jax.experimental import pallas as pl
from jax.experimental.pallas import tpu as pltpu
from jax.sharding import PartitionSpec as P

GROUP = 64
PRE = 16
HEAD = 8
NS = 40
SP = 48
NH = 16
LAT = 512
VD = 128
SUF = 384
WIN = 80
NSLOT = 5
NPROMPT = 10
NBUF = 4
MASKED = -1e30
GROUPS = ((0, 16, 0), (16, 32, 128), (48, 32, 384))
SCALE2 = math.log2(math.e) / math.sqrt(192.0)

BF = jnp.bfloat16
F32 = jnp.float32
MESH = pl.DeviceIdType.MESH


def nt(a, b):
    return lax.dot_general(a, b, (((1,), (1,)), ((), ())), preferred_element_type=F32)


def nn(a, b):
    return lax.dot_general(a, b, (((1,), (0,)), ((), ())), preferred_element_type=F32)


def onehot(mask):
    return jnp.where(mask, 1.0, 0.0).astype(BF)


def iota(shape, dim):
    return lax.broadcasted_iota(jnp.int32, shape, dim)


def kernel(
    q_hbm, k_hbm, suf_hbm, vm_hbm, w_hbm, prompts, slots, lens,
    out,
    q_in, vm, w_in, sufbuf,
    tmat, q_t, qr, krl, krr,
    skl, skr, sq, qw, kw, rank_row, rank_col, sort, unsort,
    lat_s, lt_s, o_s, l_s, osr, lsr, lacc_s,
    ol, op, lps, orr, lr, lacc,
    suf_rhs, suf, hbuf, part_o, pb, cb, xb, rs,
    ld_sem, suf_sem, a2a_s, a2a_r, x_s, x_r, c_s, c_r, g1_s, g1_r, g2_s, g2_r, e_s, e_r,
):
    p = lax.axis_index("pre")
    h = lax.axis_index("head")
    x, c = h // 2, lax.rem(h, 2)
    y, z = p // 4, lax.rem(p, 4)
    win, half = p // 2, lax.rem(p, 2)
    wj = lax.rem(win, 4)

    def remote(src, dst, ssem, rsem, pre, head):
        return pltpu.make_async_remote_copy(
            src_ref=src, dst_ref=dst, send_sem=ssem, recv_sem=rsem,
            device_id={"pre": pre, "head": head}, device_id_type=MESH,
        )

    def around(fn):
        def body(d, carry):
            fn(lax.rem(p + d, PRE))
            return carry
        lax.fori_loop(1, PRE, body, 0)

    def lane(i):
        return pl.ds(pl.multiple_of(i * 128, 128), 128)

    load_q = pltpu.make_async_copy(q_hbm, q_in, ld_sem.at[4])
    load_v = pltpu.make_async_copy(vm_hbm, vm, ld_sem.at[2])
    load_w = pltpu.make_async_copy(w_hbm, w_in, ld_sem.at[3])
    load_q.start()

    def suf_load(n, slot):
        return pltpu.make_async_copy(suf_hbm.at[n], sufbuf.at[slot], suf_sem.at[slot])

    barrier = pltpu.get_barrier_semaphore()

    def greet_pre(other):
        pl.semaphore_signal(barrier, inc=1, device_id={"pre": other, "head": h}, device_id_type=MESH)

    around(greet_pre)

    def greet_head(d, carry):
        pl.semaphore_signal(
            barrier, inc=1, device_id={"pre": p, "head": lax.rem(h + d, HEAD)}, device_id_type=MESH
        )
        return carry

    lax.fori_loop(1, HEAD, greet_head, 0)

    lacc_s[...] = jnp.zeros_like(lacc_s)
    lacc[...] = jnp.zeros_like(lacc)

    pl.semaphore_wait(barrier, PRE - 1 + HEAD - 1)

    def tiles(i):
        return (
            k_hbm.at[:, pl.ds(pl.multiple_of(c * 256 + i * 16, 16), 16), lane(x)],
            k_hbm.at[:, pl.ds(pl.multiple_of(LAT + lax.rem(i, 4) * 16, 16), 16), lane(x)],
        )

    def s1l(other, src):
        return remote(tiles(other)[0], krl.at[pl.ds(src * NSLOT, NSLOT)],
                      a2a_s.at[0, other], a2a_r.at[0, src], other, h)

    def s1r(other, src):
        return remote(tiles(other)[1], krr.at[pl.ds(src * NSLOT, NSLOT)],
                      a2a_s.at[1, other], a2a_r.at[1, src], other, h)

    def on_core0(fn):
        pl.when(c == 0)(lambda: around(fn))

    around(lambda other: s1l(other, p).start())
    on_core0(lambda other: s1r(other, p).start())
    own_l = pltpu.make_async_copy(tiles(p)[0], krl.at[pl.ds(p * NSLOT, NSLOT)], ld_sem.at[0])
    own_r = pltpu.make_async_copy(tiles(p)[1], krr.at[pl.ds(p * NSLOT, NSLOT)], ld_sem.at[1])
    own_l.start()
    own_r.start()

    def build_t(i, carry):
        row = iota((SP, NS * NH), 0)
        col = iota((SP, NS * NH), 1)
        tmat[i] = onehot((lax.shift_right_logical(col, 4) == row) & ((col & 15) == i))
        return carry

    lax.fori_loop(0, NH, build_t, 0)

    load_q.wait()
    q_flat = q_in[...].reshape(NS * NH, LAT + 64)
    for g in range(2):
        t_part = tmat[g * 8:(g + 1) * 8].reshape(8 * SP, NS * NH)
        q_t[g * 8:(g + 1) * 8] = nn(t_part, q_flat).astype(BF).reshape(8, SP, LAT + 64)
    pieces = [jnp.full((1, 128), -4, jnp.int32) for _ in range(PRE * SP // 128)]
    for n in range(PRE * NS):
        tile, at = divmod(n // NS * SP + n % NS, 128)
        pieces[tile] = jnp.where(iota((1, 128), 1) == at, prompts[n], pieces[tile])
    prompt_row = jnp.concatenate(pieces, axis=1)
    names = jnp.broadcast_to(prompt_row, (SP, PRE * SP))
    at = iota((SP, PRE * SP), 1)
    rank_row[...] = prompt_row * GROUP

    def build_rank(i, carry):
        ids = iota((SP, PRE * SP), 0) + i * SP
        name = jnp.sum(jnp.where(at == ids, names, 0), axis=1, keepdims=True)
        same = names == name
        before = jnp.sum(jnp.where(same & (at < ids), 1, 0), axis=1, keepdims=True)
        rank_col[pl.ds(pl.multiple_of(i * NS, 8), NS)] = (name * GROUP + before)[:NS]
        rank_row[...] += jnp.sum(jnp.where(same & (ids < at), 1, 0), axis=0, keepdims=True)
        return carry

    lax.fori_loop(0, PRE, build_rank, 0)
    def rank_of(place):
        r0 = 80 * lax.shift_right_logical(place, 4) + (place & 15)
        r1 = 80 * lax.shift_right_logical(place - 128, 5) + (place & 31) + 16
        r2 = 80 * lax.shift_right_logical(place - 384, 5) + (place & 31) + 48
        return jnp.where(place < 128, r0, jnp.where(place < 384, r1, r2))

    def build_sort(i, carry):
        rows = pl.ds(pl.multiple_of(i * 64, 64), 64)
        place = iota((64, 1), 0) + i * 64
        sort[rows] = onehot(rank_of(place) == rank_row[...])
        unsort[rows] = onehot(rank_col[rows] == rank_of(iota((1, PRE * NS), 1)))
        return carry

    lax.fori_loop(0, PRE * NS // 64, build_sort, 0)

    load_v.start()
    load_w.start()
    for n in range(NBUF):
        suf_load(n, n).start()

    def suffix_pair(pair, carry):
        ns = (2 * pair, 2 * pair + 1)
        slots_of = [lax.rem(n, NBUF) for n in ns]
        for n, slot in zip(ns, slots_of):
            suf_load(n, slot).wait()
        keys = [sufbuf[slot] for slot in slots_of]
        ts = [nn(q_in[n], kn) * SCALE2 for n, kn in zip(ns, keys)]
        ts = [jnp.where(iota((NH, SUF), 1) < lens[n], t, MASKED) for n, t in zip(ns, ts)]
        ms = [jnp.max(t, axis=1, keepdims=True) for t in ts]
        ws = [jnp.exp2(t - m).astype(BF) for t, m in zip(ts, ms)]
        totals = [jnp.sum(w.astype(F32), axis=1, keepdims=True) for w in ws]
        outs = [nt(w, kn[:LAT]) for w, kn in zip(ws, keys)]
        both = jnp.concatenate([o / total for o, total in zip(outs, totals)], axis=0)
        lat_s[pl.ds(pl.multiple_of(pair * 2 * NH, 2 * NH), 2 * NH)] = both.astype(BF)
        at = iota((NH, 128), 1)
        lse = [m + jnp.log2(total) for m, total in zip(ms, totals)]
        lacc_s[...] = jnp.where(at == ns[0], lse[0], jnp.where(at == ns[1], lse[1], lacc_s[...]))

        @pl.when(ns[0] + NBUF < NS)
        def _():
            for n, slot in zip(ns, slots_of):
                suf_load(n + NBUF, slot).start()

        return carry

    def suffix(first, last):
        lax.fori_loop(first // 2, last // 2, suffix_pair, 0)

    around(lambda other: s1l(other, other).wait_recv())
    on_core0(lambda other: s1r(other, other).wait_recv())
    own_l.wait()
    own_r.wait()

    def pick(prompt, carry):
        for b in range(8):
            slot = slots[b, prompt]
            skl[b // 4, prompt * 4 + b % 4] = krl[slot]
        for hf in range(2):
            skr[hf, prompt] = krr[slots[hf * 4 + p // 4, prompt]]
        return carry

    lax.fori_loop(0, NPROMPT, pick, 0)

    def first_of(other):
        return 5 * (other // 8) + lax.rem(other // 2, 4)

    def s2l(ab, other, src):
        rows = pl.ds(pl.multiple_of(c * 256 + src * 16, 16), 16)
        return remote(skl.at[lax.rem(other, 2), pl.ds((first_of(other) + ab) * 4, 4)],
                      kw.at[pl.ds(ab * 4, 4), rows, lane(x)],
                      a2a_s.at[3 + ab, other], a2a_r.at[3 + ab, src], other, h)

    def s2r(other, src):
        rows = pl.ds(pl.multiple_of(LAT + lax.rem(src, 4) * 16, 16), 16)
        return remote(skr.at[lax.rem(other, 2), pl.ds(first_of(other), 2)],
                      kw.reshape(2, 4, LAT + 64, 512).at[:, src // 4, rows, lane(x)],
                      a2a_s.at[5, other], a2a_r.at[5, src], other, h)

    own = first_of(p)
    for ab in range(2):
        around(lambda other: s2l(ab, other, p).start())
        if ab == 0:
            on_core0(lambda other: s2r(other, p).start())
    kw[:, pl.ds(pl.multiple_of(c * 256 + p * 16, 16), 16), lane(x)] = skl[half, pl.ds(own * 4, 8)]

    @pl.when(c == 0)
    def _():
        rows = pl.ds(pl.multiple_of(LAT + lax.rem(p, 4) * 16, 16), 16)
        kw[p // 4, rows, lane(x)] = skr[half, own]
        kw[p // 4 + 4, rows, lane(x)] = skr[half, own + 1]

    def s1q(other, src):
        return remote(q_t.at[other], qr.at[src], a2a_s.at[2, other], a2a_r.at[2, src], other, h)

    around(lambda other: s1q(other, p).start())
    qr[p] = q_t[p]

    suffix(0, 6)

    def views(cc, src_x):
        rows = pl.ds(pl.multiple_of(cc * 256, 256), 256)
        return kw.at[0:4, rows, lane(src_x)], kw.at[4:8, rows, lane(src_x)], kw.at[:, LAT:, lane(src_x)]

    def back(d):
        return lax.rem(x + 4 - d, 4)

    def x_copy(k, d, src_x):
        step = d if d != 2 or k == 2 else (1, 3)[k]
        view = views(c, src_x)[k]
        return remote(view, view, x_s.at[k, d - 1], x_r.at[k, d - 1], p, lax.rem(x + step, 4) * 2 + c)

    def core_copy(k, d, src_x, cc):
        view = views(cc, src_x)[k]
        return remote(view, view, c_s.at[k, d], c_r.at[k, d], p, x * 2 + (1 - c))

    def send_x(k):
        for d in (1, 3) if k < 2 else (1, 3, 2):
            x_copy(k, d, x).start()
        core_copy(k, 0, x, c).start()

    def pass_on(k, d):
        x_copy(k, d, back(d)).wait_recv()
        if (k, d) in ((0, 1), (1, 3)):
            x_copy(k, 2, back(d)).start()
        core_copy(k, d, back(d), c).start()

    def wait_core(k):
        for d in (0, 1, 3, 2):
            core_copy(k, d, back(d), 1 - c).wait_recv()

    def core0(fn):
        pl.when(c == 0)(fn)

    around(lambda other: s2l(0, other, other).wait_recv())
    send_x(0)
    on_core0(lambda other: s2r(other, other).wait_recv())
    core0(lambda: send_x(2))
    around(lambda other: s2l(1, other, other).wait_recv())
    send_x(1)
    suffix(6, 12)
    pass_on(0, 1)
    pass_on(0, 3)
    suffix(12, 18)

    around(lambda other: s1q(other, other).wait_recv())
    q_all = qr[...].reshape(PRE * SP, LAT + 64)

    def s2q(g, other, src):
        r0, nr, base = GROUPS[g]
        return remote(sq.at[pl.ds(pl.multiple_of(base + (other // 2) * nr, 16), nr)], qw.at[src, pl.ds(r0, nr)],
                      a2a_s.at[6 + g, other], a2a_r.at[6 + g, src], other, h)

    for g, (r0, nr, base) in enumerate(GROUPS):
        sq[base:base + 8 * nr] = nn(sort[base:base + 8 * nr], q_all).astype(BF)
        if g == 0:
            around(lambda other: s2q(g, other, p).start())
        qw[p, r0:r0 + nr] = sq[pl.ds(pl.multiple_of(base + win * nr, 16), nr)]

    @core0
    def _():
        for d in (1, 3, 2):
            pass_on(2, d)

    def next_group(g):
        around(lambda other: s2q(g - 1, other, p).wait_send())
        around(lambda other: s2q(g, other, p).start())

    pass_on(1, 3)
    suffix(18, 22)
    next_group(1)
    suffix(22, 26)
    pass_on(0, 2)
    pass_on(1, 1)
    suffix(26, 34)
    next_group(2)
    suffix(34, NS)

    def s4o(other, src):
        return remote(o_s.at[other], osr.at[src], a2a_s.at[9, other], a2a_r.at[9, src], other, h)

    def s4l(other, src):
        return remote(l_s.at[other], lsr.at[src], a2a_s.at[10, other], a2a_r.at[10, src], other, h)

    def start4(other):
        s4o(other, p).start()
        s4l(other, p).start()

    def spread(src, carry):
        rows = pl.ds(pl.multiple_of(src * SP, 16), SP)
        suf_rhs[rows, :VD] = osr[src]
        row = jnp.broadcast_to(lsr[src], (SP, 128))
        at = iota((SP, 128), 1)
        lse = jnp.sum(jnp.where(iota((SP, 128), 0) == at, row, 0.0), axis=1, keepdims=True)
        high = lse.astype(BF).astype(F32)
        middle = (lse - high).astype(BF).astype(F32)
        low = lse - high - middle
        terms = jnp.where(at == 0, high, jnp.where(at == 1, middle, jnp.where(at == 2, low, 0.0)))
        suf_rhs[rows, VD:] = terms.astype(BF)
        return carry

    def sort_suffix():
        def wait4(other):
            s4o(other, other).wait_recv()
            s4l(other, other).wait_recv()

        around(wait4)
        lax.fori_loop(0, PRE, spread, 0)
        suf[...] = nn(sort[...], suf_rhs[...])

    def chunk(g, t, carry):
        rows = pl.ds(pl.multiple_of(t * 16, 16), 16)
        ab = (t + wj) // 4
        qc = qw[:, rows].reshape(256, LAT + 64)
        scores = [nn(qc, kw[ab * 4 + b]) * SCALE2 for b in range(4)]
        m = functools.reduce(jnp.maximum, [jnp.max(t, axis=1, keepdims=True) for t in scores])
        total = jnp.zeros((256, 1), F32)
        acc = jnp.zeros((256, LAT), F32)
        for b in range(4):
            w = jnp.exp2(scores[b] - m).astype(BF)
            total = total + jnp.sum(w.astype(F32), axis=1, keepdims=True)
            acc = acc + nt(w, kw[ab * 4 + b, :LAT])
        ol[:, rows] = (acc / total).astype(BF).reshape(NH, 16, LAT)
        lse = (m + jnp.log2(total)).reshape(NH, 16, 1)
        here = iota((NH, 16, 128), 2) == iota((NH, 16, 128), 1) + (t * 16 - GROUPS[g][0])
        lacc[g] += jnp.sum(jnp.where(here, lse, 0.0), axis=1)
        return carry

    def s5o(g, other, src):
        r0, nr, base = GROUPS[g]
        rows = pl.ds(pl.multiple_of(base + (src // 2) * nr, 16), nr)
        return remote(op.at[other, pl.ds(r0, nr)], orr.at[rows, lane(lax.rem(src, 2))],
                      a2a_s.at[11 + g, other], a2a_r.at[11 + g, src], other, h)

    def s5l(g, other, src):
        return remote(lps.at[g, other], lr.at[g, lax.rem(src, 2), src // 2],
                      a2a_s.at[14 + g, other], a2a_r.at[14 + g, src], other, h)

    def attend(g):
        r0, nr, base = GROUPS[g]
        around(lambda other: s2q(g, other, other).wait_recv())
        lax.fori_loop(r0 // 16, (r0 + nr) // 16, functools.partial(chunk, g), 0)
        lps[g] = lacc[g][:, None, :]

        for i in range(NH):
            op[i, r0:r0 + nr] = nn(ol[i, r0:r0 + nr], vm[i]).astype(BF)

        def start5(other):
            s5o(g, other, p).start()
            s5l(g, other, p).start()

        around(start5)
        orr[pl.ds(pl.multiple_of(base + win * nr, 16), nr), lane(half)] = op[p, r0:r0 + nr]
        lr[g, half, win] = lps[g, p]

    def merge(g):
        r0, nr, base = GROUPS[g]

        def wait5(other):
            s5o(g, other, other).wait_recv()
            s5l(g, other, other).wait_recv()

        around(wait5)
        rows = slice(base, base + 8 * nr)
        eye = iota((8, nr, 128), 2) == iota((8, nr, 128), 1)

        def column(hf):
            spread_l = jnp.where(eye, jnp.broadcast_to(lr[g, hf], (8, nr, 128)), 0.0)
            return jnp.sum(spread_l, axis=2, keepdims=True).reshape(8 * nr, 1)

        la, lb = column(0), column(1)
        ls = jnp.sum(suf[rows, VD:], axis=1, keepdims=True)
        top = jnp.maximum(jnp.maximum(la, lb), ls)
        ea, eb, es = jnp.exp2(la - top), jnp.exp2(lb - top), jnp.exp2(ls - top)
        inv = 1.0 / (ea + eb + es)
        merged = (
            (ea * inv) * orr[rows, :VD].astype(F32)
            + (eb * inv) * orr[rows, VD:].astype(F32)
            + (es * inv) * suf[rows, :VD]
        )
        hbuf[y, z, rows] = merged.astype(BF)

    def half_rows(g, part):
        _, nr, base = GROUPS[g]
        return pl.ds(base + part * 4 * nr, 4 * nr)

    def first(g, part, d, src_y, src_z):
        dy, dz = (0, d) if part == 0 else (d, 0)
        view = hbuf.at[src_y, src_z, half_rows(g, part)]
        return remote(view, view, g1_s.at[g, part, d - 1], g1_r.at[g, part, d - 1],
                      lax.rem(y + dy, 4) * 4 + lax.rem(z + dz, 4), h)

    def second(g, part, d, src):
        rows = half_rows(g, part)
        dy, dz = (d, 0) if part == 0 else (0, d)
        view = hbuf.at[src, :, rows] if part == 0 else hbuf.at[:, src, rows]
        return remote(view, view, g2_s.at[g, part, d - 1], g2_r.at[g, part, d - 1],
                      lax.rem(y + dy, 4) * 4 + lax.rem(z + dz, 4), h)

    def gather1(g):
        for d in (2, 1, 3):
            for part in range(2):
                first(g, part, d, y, z).start()

    def gather2(g):
        for part in range(2):
            for d in (1, 3, 2):
                at_z = lax.rem(z + 4 - d, 4) if part == 0 else z
                at_y = lax.rem(y + 4 - d, 4) if part == 1 else y
                first(g, part, d, at_y, at_z).wait_recv()
            for d in (2, 1, 3):
                second(g, part, d, (y, z)[part]).start()

    def gathered(g):
        for d in (1, 3, 2):
            for part in range(2):
                second(g, part, d, lax.rem((y, z)[part] + 4 - d, 4)).wait_recv()

    def out_rows(g):
        _, nr, base = GROUPS[g]
        rows = slice(base, base + 8 * nr)
        merged = jnp.concatenate([hbuf[k // 4, k % 4, rows] for k in range(PRE)], axis=1)
        part_o[rows] = nt(merged, w_in[...]).astype(BF)

    pass_on(1, 2)
    wait_core(0)
    pl.when(c == 1)(lambda: wait_core(2))
    load_v.wait()
    attend(0)
    for g in range(2):
        t_part = tmat[g * 8:(g + 1) * 8].reshape(8 * SP, NS * NH)
        lt_s[g * 8:(g + 1) * 8] = nn(t_part, lat_s[...]).astype(BF).reshape(8, SP, LAT)

    for i in range(NH):
        o_s[i] = nn(lt_s[i], vm[i]).astype(BF)
    l_s[...] = lacc_s[...][:, None, :]

    around(start4)
    osr[p] = o_s[p]
    lsr[p] = l_s[p]

    wait_core(1)
    attend(1)
    sort_suffix()
    merge(0)
    gather1(0)
    attend(2)
    gather2(0)
    merge(1)
    gather1(1)
    merge(2)
    gather1(2)
    gather2(1)
    load_w.wait()
    gathered(0)
    out_rows(0)
    gather2(2)
    gathered(1)
    out_rows(1)
    gathered(2)
    out_rows(2)

    for g in range(2):
        rows = nn(unsort[g * 320:(g + 1) * 320], part_o[...]).astype(BF)
        for k in range(4):
            pb[k % 2, g * 2 + k // 2] = rows[k * WIN:(k + 1) * WIN]
    swap = remote(pb.at[1 - c], cb, e_s.at[0], e_r.at[0], p, x * 2 + (1 - c))
    swap.start()
    swap.wait_recv()

    def s6(d, src_x):
        to = lax.rem(x + d, 4)
        return remote(xb.at[to], rs.at[src_x], e_s.at[d], e_r.at[d], p, to * 2 + c)

    for d in (2, 1, 3):
        to = lax.rem(x + d, 4)
        xb[to] = (pb[c, to].astype(F32) + cb[to].astype(F32)).astype(BF)
        s6(d, x).start()
    def sent(other):
        for copy in (s1l, s1q, s4o, s4l):
            copy(other, p).wait_send()
        for ab in range(2):
            s2l(ab, other, p).wait_send()
        for g in range(3):
            for copy in (s5o, s5l):
                copy(g, other, p).wait_send()
        s2q(2, other, p).wait_send()

    around(sent)
    on_core0(lambda other: s1r(other, p).wait_send())
    on_core0(lambda other: s2r(other, p).wait_send())

    def sent_blocks(k):
        for d in (1, 2, 3):
            x_copy(k, d, x).wait_send()
        for d in range(4):
            core_copy(k, d, back(d), c).wait_send()

    sent_blocks(0)
    sent_blocks(1)
    core0(lambda: sent_blocks(2))
    for g in range(3):
        for part in range(2):
            for d in (1, 2, 3):
                first(g, part, d, y, z).wait_send()
                second(g, part, d, (y, z)[part]).wait_send()

    total = pb[c, x].astype(F32) + cb[x].astype(F32)
    for d in (1, 3, 2):
        s6(d, back(d)).wait_recv()
        total = total + rs[back(d)].astype(F32)
    out[...] = total.astype(BF)

    swap.wait_send()
    for d in (1, 2, 3):
        s6(d, x).wait_send()


def per_device(
    query_latent, prefix_cache, block_slot, sample_prompt, suffix_cache, suffix_length, value_map, out_weight
):
    vmem = pl.BlockSpec(memory_space=pltpu.VMEM)
    smem = pl.BlockSpec(memory_space=pltpu.SMEM)
    hbm = pl.BlockSpec(memory_space=pl.ANY)
    V = pltpu.VMEM
    dma = pltpu.SemaphoreType.DMA
    width = LAT + 64
    scratch = [
        V((NS, NH, width), BF), V((NH, LAT, VD), BF), V((448, NH * VD), BF),
        V((NBUF, width, SUF), BF),
        V((NH, SP, NS * NH), BF), V((NH, SP, width), BF), V((PRE, SP, width), BF),
        V((PRE * NSLOT, 16, 128), BF), V((PRE * NSLOT, 16, 128), BF),
        V((2, NPROMPT * 4, 16, 128), BF), V((2, NPROMPT, 16, 128), BF),
        V((PRE * NS, width), BF), V((NH, WIN, width), BF),
        V((8, width, 512), BF), V((1, PRE * SP), jnp.int32), V((PRE * NS, 1), jnp.int32),
        V((PRE * NS, PRE * SP), BF), V((PRE * NS, PRE * NS), BF),
        V((NS * NH, LAT), BF), V((NH, SP, LAT), BF), V((NH, SP, VD), BF), V((NH, 1, 128), F32),
        V((PRE, SP, VD), BF), V((PRE, 1, 128), F32), V((NH, 128), F32),
        V((NH, WIN, LAT), BF), V((NH, WIN, VD), BF), V((3, NH, 1, 128), F32),
        V((PRE * NS, 2 * VD), BF), V((3, 2, 8, 1, 128), F32), V((3, NH, 128), F32),
        V((PRE * SP, 2 * VD), BF), V((PRE * NS, 2 * VD), F32), V((4, 4, PRE * NS, VD), BF),
        V((PRE * NS, 448), BF), V((2, 4, WIN, 448), BF), V((4, WIN, 448), BF), V((4, WIN, 448), BF), V((4, WIN, 448), BF),
        dma((5,)), dma((NBUF,)), dma((17, PRE)), dma((17, PRE)),
        dma((3, 3)), dma((3, 3)), dma((3, 4)), dma((3, 4)),
        dma((3, 2, 3)), dma((3, 2, 3)), dma((3, 2, 3)), dma((3, 2, 3)), dma((4,)), dma((4,)),
    ]
    return pl.pallas_call(
        kernel,
        out_shape=jax.ShapeDtypeStruct((WIN, 448), BF),
        in_specs=[hbm, hbm, hbm, hbm, hbm, smem, smem, smem],
        out_specs=vmem,
        scratch_shapes=scratch,
        compiler_params=pltpu.CompilerParams(
            collective_id=0, has_side_effects=True, vmem_limit_bytes=58 * 1024 * 1024
        ),
        cost_estimate=pl.CostEstimate(flops=10_000_000_000, bytes_accessed=30_000_000, transcendentals=3_000_000),
    )(
        query_latent, prefix_cache.transpose(0, 2, 1), suffix_cache.transpose(0, 2, 1), value_map, out_weight.T,
        sample_prompt, block_slot.T, suffix_length,
    )


def solution(mesh):
    return jax.shard_map(
        per_device,
        mesh=mesh,
        in_specs=(
            P("pre", "head", None),
            P("pre", None, None),
            P(),
            P(),
            P("pre", None, None),
            P("pre"),
            P("head", None, None),
            P("head", "pre"),
        ),
        out_specs=P("head", "pre"),
        check_vma=False,
    )
```

```python
import functools
import math

import jax
import jax.numpy as jnp
from jax import lax
from jax.experimental import pallas as pl
from jax.experimental.pallas import tpu as pltpu
from jax.sharding import PartitionSpec as P

GROUP = 64
PRE = 16
HEAD = 8
NS = 40
SP = 48
NH = 16
LAT = 512
VD = 128
SUF = 384
WIN = 80
NSLOT = 5
NPROMPT = 10
NBUF = 4
MASKED = -1e30
GROUPS = ((0, 16, 0), (16, 32, 128), (48, 32, 384))
SCALE2 = math.log2(math.e) / math.sqrt(192.0)

BF = jnp.bfloat16
F32 = jnp.float32
MESH = pl.DeviceIdType.MESH


def nt(a, b):
    return lax.dot_general(a, b, (((1,), (1,)), ((), ())), preferred_element_type=F32)


def nn(a, b):
    return lax.dot_general(a, b, (((1,), (0,)), ((), ())), preferred_element_type=F32)


def onehot(mask):
    return jnp.where(mask, 1.0, 0.0).astype(BF)


def iota(shape, dim):
    return lax.broadcasted_iota(jnp.int32, shape, dim)


def kernel(
    q_hbm, k_hbm, suf_hbm, vm_hbm, w_hbm, prompts, slots, lens,
    out,
    q_in, vm, w_in, sufbuf,
    tmat, q_t, qr, krl, krr,
    skl, skr, sq, qw, kw, rank_row, rank_col, sort, unsort,
    lat_s, lt_s, o_s, l_s, osr, lsr, lacc_s,
    ol, op, lps, orr, lr, lacc,
    suf_rhs, suf, hbuf, part_o, pb, cb, xb, rs,
    ld_sem, suf_sem, a2a_s, a2a_r, x_s, x_r, c_s, c_r, g1_s, g1_r, g2_s, g2_r, e_s, e_r,
):
    p = lax.axis_index("pre")
    h = lax.axis_index("head")
    x, c = h // 2, lax.rem(h, 2)
    y, z = p // 4, lax.rem(p, 4)
    win, half = p // 2, lax.rem(p, 2)
    wj = lax.rem(win, 4)

    def remote(src, dst, ssem, rsem, pre, head):
        return pltpu.make_async_remote_copy(
            src_ref=src, dst_ref=dst, send_sem=ssem, recv_sem=rsem,
            device_id={"pre": pre, "head": head}, device_id_type=MESH,
        )

    def around(fn):
        def body(d, carry):
            fn(lax.rem(p + d, PRE))
            return carry
        lax.fori_loop(1, PRE, body, 0)

    def lane(i):
        return pl.ds(pl.multiple_of(i * 128, 128), 128)

    load_q = pltpu.make_async_copy(q_hbm, q_in, ld_sem.at[4])
    load_v = pltpu.make_async_copy(vm_hbm, vm, ld_sem.at[2])
    load_w = pltpu.make_async_copy(w_hbm, w_in, ld_sem.at[3])
    load_q.start()

    def suf_load(n, slot):
        return pltpu.make_async_copy(suf_hbm.at[n], sufbuf.at[slot], suf_sem.at[slot])

    barrier = pltpu.get_barrier_semaphore()

    def greet_pre(other):
        pl.semaphore_signal(barrier, inc=1, device_id={"pre": other, "head": h}, device_id_type=MESH)

    around(greet_pre)

    def greet_head(d, carry):
        pl.semaphore_signal(
            barrier, inc=1, device_id={"pre": p, "head": lax.rem(h + d, HEAD)}, device_id_type=MESH
        )
        return carry

    lax.fori_loop(1, HEAD, greet_head, 0)

    lacc_s[...] = jnp.zeros_like(lacc_s)
    lacc[...] = jnp.zeros_like(lacc)

    pl.semaphore_wait(barrier, PRE - 1 + HEAD - 1)

    def tiles(i):
        return (
            k_hbm.at[:, pl.ds(pl.multiple_of(c * 256 + i * 16, 16), 16), lane(x)],
            k_hbm.at[:, pl.ds(pl.multiple_of(LAT + lax.rem(i, 4) * 16, 16), 16), lane(x)],
        )

    def s1l(other, src):
        return remote(tiles(other)[0], krl.at[pl.ds(src * NSLOT, NSLOT)],
                      a2a_s.at[0, other], a2a_r.at[0, src], other, h)

    def s1r(other, src):
        return remote(tiles(other)[1], krr.at[pl.ds(src * NSLOT, NSLOT)],
                      a2a_s.at[1, other], a2a_r.at[1, src], other, h)

    def on_core0(fn):
        pl.when(c == 0)(lambda: around(fn))

    around(lambda other: s1l(other, p).start())
    on_core0(lambda other: s1r(other, p).start())
    own_l = pltpu.make_async_copy(tiles(p)[0], krl.at[pl.ds(p * NSLOT, NSLOT)], ld_sem.at[0])
    own_r = pltpu.make_async_copy(tiles(p)[1], krr.at[pl.ds(p * NSLOT, NSLOT)], ld_sem.at[1])
    own_l.start()
    own_r.start()

    def build_t(i, carry):
        row = iota((SP, NS * NH), 0)
        col = iota((SP, NS * NH), 1)
        tmat[i] = onehot((lax.shift_right_logical(col, 4) == row) & ((col & 15) == i))
        return carry

    lax.fori_loop(0, NH, build_t, 0)

    load_q.wait()
    q_flat = q_in[...].reshape(NS * NH, LAT + 64)
    for g in range(2):
        t_part = tmat[g * 8:(g + 1) * 8].reshape(8 * SP, NS * NH)
        q_t[g * 8:(g + 1) * 8] = nn(t_part, q_flat).astype(BF).reshape(8, SP, LAT + 64)
    pieces = [jnp.full((1, 128), -4, jnp.int32) for _ in range(PRE * SP // 128)]
    for n in range(PRE * NS):
        tile, at = divmod(n // NS * SP + n % NS, 128)
        pieces[tile] = jnp.where(iota((1, 128), 1) == at, prompts[n], pieces[tile])
    prompt_row = jnp.concatenate(pieces, axis=1)
    names = jnp.broadcast_to(prompt_row, (SP, PRE * SP))
    at = iota((SP, PRE * SP), 1)
    rank_row[...] = prompt_row * GROUP

    def build_rank(i, carry):
        ids = iota((SP, PRE * SP), 0) + i * SP
        name = jnp.sum(jnp.where(at == ids, names, 0), axis=1, keepdims=True)
        same = names == name
        before = jnp.sum(jnp.where(same & (at < ids), 1, 0), axis=1, keepdims=True)
        rank_col[pl.ds(pl.multiple_of(i * NS, 8), NS)] = (name * GROUP + before)[:NS]
        rank_row[...] += jnp.sum(jnp.where(same & (ids < at), 1, 0), axis=0, keepdims=True)
        return carry

    lax.fori_loop(0, PRE, build_rank, 0)
    def rank_of(place):
        w = jnp.where(
            place < 128, lax.shift_right_logical(place, 4),
            jnp.where(place < 384, lax.shift_right_logical(place - 128, 5), lax.shift_right_logical(place - 384, 5)),
        )
        u = jnp.where(place < 128, place & 15, jnp.where(place < 384, (place & 31) + 16, (place & 31) + 48))
        return 80 * w + jnp.where((w & 3) < 2, u, 64 - u + 2 * (u & 15))

    def build_sort(i, carry):
        rows = pl.ds(pl.multiple_of(i * 64, 64), 64)
        place = iota((64, 1), 0) + i * 64
        sort[rows] = onehot(rank_of(place) == rank_row[...])
        unsort[rows] = onehot(rank_col[rows] == rank_of(iota((1, PRE * NS), 1)))
        return carry

    lax.fori_loop(0, PRE * NS // 64, build_sort, 0)

    load_v.start()
    load_w.start()
    for n in range(NBUF):
        suf_load(n, n).start()

    def suffix_pair(pair, carry):
        ns = (2 * pair, 2 * pair + 1)
        slots_of = [lax.rem(n, NBUF) for n in ns]
        for n, slot in zip(ns, slots_of):
            suf_load(n, slot).wait()
        keys = [sufbuf[slot] for slot in slots_of]
        ts = [nn(q_in[n], kn) * SCALE2 for n, kn in zip(ns, keys)]
        ts = [jnp.where(iota((NH, SUF), 1) < lens[n], t, MASKED) for n, t in zip(ns, ts)]
        ms = [jnp.max(t, axis=1, keepdims=True) for t in ts]
        ws = [jnp.exp2(t - m).astype(BF) for t, m in zip(ts, ms)]
        totals = [jnp.sum(w.astype(F32), axis=1, keepdims=True) for w in ws]
        outs = [nt(w, kn[:LAT]) for w, kn in zip(ws, keys)]
        both = jnp.concatenate([o / total for o, total in zip(outs, totals)], axis=0)
        lat_s[pl.ds(pl.multiple_of(pair * 2 * NH, 2 * NH), 2 * NH)] = both.astype(BF)
        at = iota((NH, 128), 1)
        lse = [m + jnp.log2(total) for m, total in zip(ms, totals)]
        lacc_s[...] = jnp.where(at == ns[0], lse[0], jnp.where(at == ns[1], lse[1], lacc_s[...]))

        @pl.when(ns[0] + NBUF < NS)
        def _():
            for n, slot in zip(ns, slots_of):
                suf_load(n + NBUF, slot).start()

        return carry

    def suffix(first, last):
        lax.fori_loop(first // 2, last // 2, suffix_pair, 0)

    around(lambda other: s1l(other, other).wait_recv())
    on_core0(lambda other: s1r(other, other).wait_recv())
    own_l.wait()
    own_r.wait()

    def pick(prompt, carry):
        for b in range(8):
            slot = slots[b, prompt]
            skl[b // 4, prompt * 4 + b % 4] = krl[slot]
        for hf in range(2):
            tile = krr[slots[hf * 4 + p // 4, prompt]]
            skr[hf, 0, prompt] = tile
            skr[hf, 1, NPROMPT - 1 - prompt] = tile
        return carry

    lax.fori_loop(0, NPROMPT, pick, 0)

    def first_of(other):
        return 5 * (other // 8) + lax.rem(other // 2, 4)

    def backwards(other):
        return lax.rem(other // 2, 4) // 2

    def rope_from(other):
        return first_of(other) + backwards(other) * (NPROMPT - 2 - 2 * first_of(other))

    def s2l(ab, other, src):
        rows = pl.ds(pl.multiple_of(c * 256 + src * 16, 16), 16)
        return remote(skl.at[lax.rem(other, 2), pl.ds((first_of(other) + lax.rem(ab + backwards(other), 2)) * 4, 4)],
                      kw.at[pl.ds(ab * 4, 4), rows, lane(x)],
                      a2a_s.at[3 + ab, other], a2a_r.at[3 + ab, src], other, h)

    def s2r(other, src):
        rows = pl.ds(pl.multiple_of(LAT + lax.rem(src, 4) * 16, 16), 16)
        return remote(skr.at[lax.rem(other, 2), backwards(other), pl.ds(rope_from(other), 2)],
                      kw.reshape(2, 4, LAT + 64, 512).at[:, src // 4, rows, lane(x)],
                      a2a_s.at[5, other], a2a_r.at[5, src], other, h)

    own = first_of(p)
    for ab in range(2):
        around(lambda other: s2l(ab, other, p).start())
        if ab == 0:
            on_core0(lambda other: s2r(other, p).start())
    for ab in range(2):
        kw[ab * 4:ab * 4 + 4, pl.ds(pl.multiple_of(c * 256 + p * 16, 16), 16), lane(x)] = skl[
            half, pl.ds((own + lax.rem(ab + backwards(p), 2)) * 4, 4)
        ]

    @pl.when(c == 0)
    def _():
        rows = pl.ds(pl.multiple_of(LAT + lax.rem(p, 4) * 16, 16), 16)
        kw[p // 4, rows, lane(x)] = skr[half, backwards(p), rope_from(p)]
        kw[p // 4 + 4, rows, lane(x)] = skr[half, backwards(p), rope_from(p) + 1]

    def s1q(other, src):
        return remote(q_t.at[other], qr.at[src], a2a_s.at[2, other], a2a_r.at[2, src], other, h)

    around(lambda other: s1q(other, p).start())
    qr[p] = q_t[p]

    suffix(0, 6)

    def views(cc, src_x):
        rows = pl.ds(pl.multiple_of(cc * 256, 256), 256)
        return kw.at[0:4, rows, lane(src_x)], kw.at[4:8, rows, lane(src_x)], kw.at[:, LAT:, lane(src_x)]

    def back(d):
        return lax.rem(x + 4 - d, 4)

    def x_copy(k, d, src_x):
        step = d if d != 2 or k == 2 else (1, 3)[k]
        view = views(c, src_x)[k]
        return remote(view, view, x_s.at[k, d - 1], x_r.at[k, d - 1], p, lax.rem(x + step, 4) * 2 + c)

    def core_copy(k, d, src_x, cc):
        view = views(cc, src_x)[k]
        return remote(view, view, c_s.at[k, d], c_r.at[k, d], p, x * 2 + (1 - c))

    def send_x(k):
        for d in (1, 3) if k < 2 else (1, 3, 2):
            x_copy(k, d, x).start()
        core_copy(k, 0, x, c).start()

    def pass_on(k, d):
        x_copy(k, d, back(d)).wait_recv()
        if (k, d) in ((0, 1), (1, 3)):
            x_copy(k, 2, back(d)).start()
        core_copy(k, d, back(d), c).start()

    def wait_core(k):
        for d in (0, 1, 3, 2):
            core_copy(k, d, back(d), 1 - c).wait_recv()

    def core0(fn):
        pl.when(c == 0)(fn)

    around(lambda other: s2l(0, other, other).wait_recv())
    send_x(0)
    on_core0(lambda other: s2r(other, other).wait_recv())
    core0(lambda: send_x(2))
    around(lambda other: s2l(1, other, other).wait_recv())
    send_x(1)
    suffix(6, 12)
    pass_on(0, 1)
    pass_on(0, 3)
    suffix(12, 18)

    around(lambda other: s1q(other, other).wait_recv())
    q_all = qr[...].reshape(PRE * SP, LAT + 64)

    def s2q(g, other, src):
        r0, nr, base = GROUPS[g]
        return remote(sq.at[pl.ds(pl.multiple_of(base + (other // 2) * nr, 16), nr)], qw.at[src, pl.ds(r0, nr)],
                      a2a_s.at[6 + g, other], a2a_r.at[6 + g, src], other, h)

    for g, (r0, nr, base) in enumerate(GROUPS):
        sq[base:base + 8 * nr] = nn(sort[base:base + 8 * nr], q_all).astype(BF)
        if g == 0:
            around(lambda other: s2q(g, other, p).start())
        qw[p, r0:r0 + nr] = sq[pl.ds(pl.multiple_of(base + win * nr, 16), nr)]

    @core0
    def _():
        for d in (1, 3, 2):
            pass_on(2, d)

    def next_group(g):
        around(lambda other: s2q(g - 1, other, p).wait_send())
        around(lambda other: s2q(g, other, p).start())

    pass_on(1, 3)
    suffix(18, 22)
    next_group(1)
    suffix(22, 26)
    pass_on(0, 2)
    pass_on(1, 1)
    suffix(26, 34)
    next_group(2)
    suffix(34, NS)

    def s4o(other, src):
        return remote(o_s.at[other], osr.at[src], a2a_s.at[9, other], a2a_r.at[9, src], other, h)

    def s4l(other, src):
        return remote(l_s.at[other], lsr.at[src], a2a_s.at[10, other], a2a_r.at[10, src], other, h)

    def start4(other):
        s4o(other, p).start()
        s4l(other, p).start()

    def spread(src, carry):
        rows = pl.ds(pl.multiple_of(src * SP, 16), SP)
        suf_rhs[rows, :VD] = osr[src]
        row = jnp.broadcast_to(lsr[src], (SP, 128))
        at = iota((SP, 128), 1)
        lse = jnp.sum(jnp.where(iota((SP, 128), 0) == at, row, 0.0), axis=1, keepdims=True)
        high = lse.astype(BF).astype(F32)
        middle = (lse - high).astype(BF).astype(F32)
        low = lse - high - middle
        terms = jnp.where(at == 0, high, jnp.where(at == 1, middle, jnp.where(at == 2, low, 0.0)))
        suf_rhs[rows, VD:] = terms.astype(BF)
        return carry

    def sort_suffix():
        def wait4(other):
            s4o(other, other).wait_recv()
            s4l(other, other).wait_recv()

        around(wait4)
        lax.fori_loop(0, PRE, spread, 0)
        suf[...] = nn(sort[...], suf_rhs[...])

    def chunk(g, t, carry):
        rows = pl.ds(pl.multiple_of(t * 16, 16), 16)
        ab = jnp.where(wj < 2, (t + wj) // 4, 1 - (4 - t + wj) // 4)
        qc = qw[:, rows].reshape(256, LAT + 64)
        scores = [nn(qc, kw[ab * 4 + b]) * SCALE2 for b in range(4)]
        m = functools.reduce(jnp.maximum, [jnp.max(t, axis=1, keepdims=True) for t in scores])
        total = jnp.zeros((256, 1), F32)
        acc = jnp.zeros((256, LAT), F32)
        for b in range(4):
            w = jnp.exp2(scores[b] - m).astype(BF)
            total = total + jnp.sum(w.astype(F32), axis=1, keepdims=True)
            acc = acc + nt(w, kw[ab * 4 + b, :LAT])
        ol[:, rows] = (acc / total).astype(BF).reshape(NH, 16, LAT)
        lse = (m + jnp.log2(total)).reshape(NH, 16, 1)
        here = iota((NH, 16, 128), 2) == iota((NH, 16, 128), 1) + (t * 16 - GROUPS[g][0])
        lacc[g] += jnp.sum(jnp.where(here, lse, 0.0), axis=1)
        return carry

    def s5o(g, other, src):
        r0, nr, base = GROUPS[g]
        rows = pl.ds(pl.multiple_of(base + (src // 2) * nr, 16), nr)
        return remote(op.at[other, pl.ds(r0, nr)], orr.at[rows, lane(lax.rem(src, 2))],
                      a2a_s.at[11 + g, other], a2a_r.at[11 + g, src], other, h)

    def s5l(g, other, src):
        return remote(lps.at[g, other], lr.at[g, lax.rem(src, 2), src // 2],
                      a2a_s.at[14 + g, other], a2a_r.at[14 + g, src], other, h)

    def attend(g):
        r0, nr, base = GROUPS[g]
        around(lambda other: s2q(g, other, other).wait_recv())
        lax.fori_loop(r0 // 16, (r0 + nr) // 16, functools.partial(chunk, g), 0)
        lps[g] = lacc[g][:, None, :]

        for i in range(NH):
            op[i, r0:r0 + nr] = nn(ol[i, r0:r0 + nr], vm[i]).astype(BF)

        def start5(other):
            s5o(g, other, p).start()
            s5l(g, other, p).start()

        around(start5)
        orr[pl.ds(pl.multiple_of(base + win * nr, 16), nr), lane(half)] = op[p, r0:r0 + nr]
        lr[g, half, win] = lps[g, p]

    def merge(g):
        r0, nr, base = GROUPS[g]

        def wait5(other):
            s5o(g, other, other).wait_recv()
            s5l(g, other, other).wait_recv()

        around(wait5)
        rows = slice(base, base + 8 * nr)
        eye = iota((8, nr, 128), 2) == iota((8, nr, 128), 1)

        def column(hf):
            spread_l = jnp.where(eye, jnp.broadcast_to(lr[g, hf], (8, nr, 128)), 0.0)
            return jnp.sum(spread_l, axis=2, keepdims=True).reshape(8 * nr, 1)

        la, lb = column(0), column(1)
        ls = jnp.sum(suf[rows, VD:], axis=1, keepdims=True)
        top = jnp.maximum(jnp.maximum(la, lb), ls)
        ea, eb, es = jnp.exp2(la - top), jnp.exp2(lb - top), jnp.exp2(ls - top)
        inv = 1.0 / (ea + eb + es)
        merged = (
            (ea * inv) * orr[rows, :VD].astype(F32)
            + (eb * inv) * orr[rows, VD:].astype(F32)
            + (es * inv) * suf[rows, :VD]
        )
        hbuf[y, z, rows] = merged.astype(BF)

    def half_rows(g, part):
        _, nr, base = GROUPS[g]
        return pl.ds(base + part * 4 * nr, 4 * nr)

    def first(g, part, d, src_y, src_z):
        dy, dz = (0, d) if part == 0 else (d, 0)
        view = hbuf.at[src_y, src_z, half_rows(g, part)]
        return remote(view, view, g1_s.at[g, part, d - 1], g1_r.at[g, part, d - 1],
                      lax.rem(y + dy, 4) * 4 + lax.rem(z + dz, 4), h)

    def second(g, part, d, src):
        rows = half_rows(g, part)
        dy, dz = (d, 0) if part == 0 else (0, d)
        view = hbuf.at[src, :, rows] if part == 0 else hbuf.at[:, src, rows]
        return remote(view, view, g2_s.at[g, part, d - 1], g2_r.at[g, part, d - 1],
                      lax.rem(y + dy, 4) * 4 + lax.rem(z + dz, 4), h)

    def gather1(g):
        for d in (2, 1, 3):
            for part in range(2):
                first(g, part, d, y, z).start()

    def gather2(g):
        for part in range(2):
            for d in (1, 3, 2):
                at_z = lax.rem(z + 4 - d, 4) if part == 0 else z
                at_y = lax.rem(y + 4 - d, 4) if part == 1 else y
                first(g, part, d, at_y, at_z).wait_recv()
            for d in (2, 1, 3):
                second(g, part, d, (y, z)[part]).start()

    def gathered(g):
        for d in (1, 3, 2):
            for part in range(2):
                second(g, part, d, lax.rem((y, z)[part] + 4 - d, 4)).wait_recv()

    def out_rows(g):
        _, nr, base = GROUPS[g]
        rows = slice(base, base + 8 * nr)
        merged = jnp.concatenate([hbuf[k // 4, k % 4, rows] for k in range(PRE)], axis=1)
        part_o[rows] = nt(merged, w_in[...]).astype(BF)

    wait_core(0)
    pl.when(c == 1)(lambda: wait_core(2))
    load_v.wait()
    attend(0)
    for g in range(2):
        t_part = tmat[g * 8:(g + 1) * 8].reshape(8 * SP, NS * NH)
        lt_s[g * 8:(g + 1) * 8] = nn(t_part, lat_s[...]).astype(BF).reshape(8, SP, LAT)

    for i in range(NH):
        o_s[i] = nn(lt_s[i], vm[i]).astype(BF)
    l_s[...] = lacc_s[...][:, None, :]

    around(start4)
    osr[p] = o_s[p]
    lsr[p] = l_s[p]

    pass_on(1, 2)
    attend(1)
    sort_suffix()
    merge(0)
    gather1(0)
    wait_core(1)
    attend(2)
    gather2(0)
    merge(1)
    gather1(1)
    merge(2)
    gather1(2)
    gather2(1)
    load_w.wait()
    gathered(0)
    out_rows(0)
    gather2(2)
    gathered(1)
    out_rows(1)
    gathered(2)
    out_rows(2)

    for g in range(2):
        rows = nn(unsort[g * 320:(g + 1) * 320], part_o[...]).astype(BF)
        for k in range(4):
            pb[k % 2, g * 2 + k // 2] = rows[k * WIN:(k + 1) * WIN]
    swap = remote(pb.at[1 - c], cb, e_s.at[0], e_r.at[0], p, x * 2 + (1 - c))
    swap.start()
    swap.wait_recv()

    def s6(d, src_x):
        to = lax.rem(x + d, 4)
        return remote(xb.at[to], rs.at[src_x], e_s.at[d], e_r.at[d], p, to * 2 + c)

    for d in (2, 1, 3):
        to = lax.rem(x + d, 4)
        xb[to] = (pb[c, to].astype(F32) + cb[to].astype(F32)).astype(BF)
        s6(d, x).start()
    def sent(other):
        for copy in (s1l, s1q, s4o, s4l):
            copy(other, p).wait_send()
        for ab in range(2):
            s2l(ab, other, p).wait_send()
        for g in range(3):
            for copy in (s5o, s5l):
                copy(g, other, p).wait_send()
        s2q(2, other, p).wait_send()

    around(sent)
    on_core0(lambda other: s1r(other, p).wait_send())
    on_core0(lambda other: s2r(other, p).wait_send())

    def sent_blocks(k):
        for d in (1, 2, 3):
            x_copy(k, d, x).wait_send()
        for d in range(4):
            core_copy(k, d, back(d), c).wait_send()

    sent_blocks(0)
    sent_blocks(1)
    core0(lambda: sent_blocks(2))
    for g in range(3):
        for part in range(2):
            for d in (1, 2, 3):
                first(g, part, d, y, z).wait_send()
                second(g, part, d, (y, z)[part]).wait_send()

    total = pb[c, x].astype(F32) + cb[x].astype(F32)
    for d in (1, 3, 2):
        s6(d, back(d)).wait_recv()
        total = total + rs[back(d)].astype(F32)
    out[...] = total.astype(BF)

    swap.wait_send()
    for d in (1, 2, 3):
        s6(d, x).wait_send()


def per_device(
    query_latent, prefix_cache, block_slot, sample_prompt, suffix_cache, suffix_length, value_map, out_weight
):
    vmem = pl.BlockSpec(memory_space=pltpu.VMEM)
    smem = pl.BlockSpec(memory_space=pltpu.SMEM)
    hbm = pl.BlockSpec(memory_space=pl.ANY)
    V = pltpu.VMEM
    dma = pltpu.SemaphoreType.DMA
    width = LAT + 64
    scratch = [
        V((NS, NH, width), BF), V((NH, LAT, VD), BF), V((448, NH * VD), BF),
        V((NBUF, width, SUF), BF),
        V((NH, SP, NS * NH), BF), V((NH, SP, width), BF), V((PRE, SP, width), BF),
        V((PRE * NSLOT, 16, 128), BF), V((PRE * NSLOT, 16, 128), BF),
        V((2, NPROMPT * 4, 16, 128), BF), V((2, 2, NPROMPT, 16, 128), BF),
        V((PRE * NS, width), BF), V((NH, WIN, width), BF),
        V((8, width, 512), BF), V((1, PRE * SP), jnp.int32), V((PRE * NS, 1), jnp.int32),
        V((PRE * NS, PRE * SP), BF), V((PRE * NS, PRE * NS), BF),
        V((NS * NH, LAT), BF), V((NH, SP, LAT), BF), V((NH, SP, VD), BF), V((NH, 1, 128), F32),
        V((PRE, SP, VD), BF), V((PRE, 1, 128), F32), V((NH, 128), F32),
        V((NH, WIN, LAT), BF), V((NH, WIN, VD), BF), V((3, NH, 1, 128), F32),
        V((PRE * NS, 2 * VD), BF), V((3, 2, 8, 1, 128), F32), V((3, NH, 128), F32),
        V((PRE * SP, 2 * VD), BF), V((PRE * NS, 2 * VD), F32), V((4, 4, PRE * NS, VD), BF),
        V((PRE * NS, 448), BF), V((2, 4, WIN, 448), BF), V((4, WIN, 448), BF), V((4, WIN, 448), BF), V((4, WIN, 448), BF),
        dma((5,)), dma((NBUF,)), dma((17, PRE)), dma((17, PRE)),
        dma((3, 3)), dma((3, 3)), dma((3, 4)), dma((3, 4)),
        dma((3, 2, 3)), dma((3, 2, 3)), dma((3, 2, 3)), dma((3, 2, 3)), dma((4,)), dma((4,)),
    ]
    return pl.pallas_call(
        kernel,
        out_shape=jax.ShapeDtypeStruct((WIN, 448), BF),
        in_specs=[hbm, hbm, hbm, hbm, hbm, smem, smem, smem],
        out_specs=vmem,
        scratch_shapes=scratch,
        compiler_params=pltpu.CompilerParams(
            collective_id=0, has_side_effects=True, vmem_limit_bytes=58 * 1024 * 1024
        ),
        cost_estimate=pl.CostEstimate(flops=10_000_000_000, bytes_accessed=30_000_000, transcendentals=3_000_000),
    )(
        query_latent, prefix_cache.transpose(0, 2, 1), suffix_cache.transpose(0, 2, 1), value_map, out_weight.T,
        sample_prompt, block_slot.T, suffix_length,
    )


def solution(mesh):
    return jax.shard_map(
        per_device,
        mesh=mesh,
        in_specs=(
            P("pre", "head", None),
            P("pre", None, None),
            P(),
            P(),
            P("pre", None, None),
            P("pre"),
            P("head", None, None),
            P("head", "pre"),
        ),
        out_specs=P("head", "pre"),
        check_vma=False,
    )
```
